256 devices in a mesh: dp: 64 (over z, x, core), layer: 4 (over y).
Axes of the slice: x: 4, y: 4, z: 8, core: 2. Of those that a mesh axis runs over, the one named last changes fastest.
Arguments:
- output_grad: bfloat16 [4, 64, 128, 7168], P('layer', None, 'dp')
- output_momentum: float32 [4, 64, 128, 7168], P('layer', None, 'dp'), may hold values from -3 to 3
- values_grad: bfloat16 [4, 64, 256, 512], P('layer', None, 'dp')
- values_momentum: float32 [4, 64, 256, 512], P('layer', None, 'dp'), may hold values from -3 to 3
- owner_table: int32 [4, 2, 64, 1], P('layer'), may hold values from 0 to 63; in each aligned block of 64 rows (0 to 63, 64 to 127, ..., all dimensions but the last counted through in order) at most 3 rows name the same one
Outputs:
- output_update: bfloat16 [4, 64, 128, 7168], P('layer', None, 'dp')
- output_next: float32 [4, 64, 128, 7168], P('layer', None, 'dp')
- values_update: bfloat16 [4, 64, 256, 512], P('layer', None, 'dp')
- values_next: float32 [4, 64, 256, 512], P('layer', None, 'dp')
- slot_rms: float32 [4, 2, 64, 3], P('layer', None, 'dp')
The draws below stay inside these ranges and needn't reach their ends.
Inputs may be any that keep to these rules, and one draw needn't show every extreme that they name: `owner_table`: for each layer and kind, no owner is named for more than 3 heads, and in some layer and kind one owner is named for exactly 3.
All inputs are finite; a program needn't handle non-finite values.
Results may differ from the reference program's by a relative error of at most 0.012.
Values may be sent and summed in bfloat16 or wider, within the bound.
No kernel may reach another device: no remote copies, remote signals or barrier semaphores. Data moves between devices by JAX's collectives and lax.ppermute only.
A program may use at most 128 MiB of HBM per device.

```python
import math
import jax
import jax.numpy as jnp
import numpy as np
from jax import lax

D = 7168
HEAD_DIM = 128
KV_OUT = 256
KV_RANK = 512
ITERS = 2
HEADS = 64
LAYERS = 4
OWNERS = 64
CAP = 3


def shape_grad(key, base):
    layers, heads, height, breadth = base.shape
    keys = jax.random.split(key, 3)
    head_scale = jnp.exp(jax.random.uniform(keys[0], (layers, heads, 1, 1), jnp.float32, -1.0, 1.0))
    row_scale = jnp.exp(jax.random.uniform(keys[1], (layers, heads, height, 1), jnp.float32, 0.0, math.log(10.0))) / 4.64
    column_scale = jnp.exp(jax.random.uniform(keys[2], (layers, heads, 1, breadth), jnp.float32, 0.0, math.log(10.0))) / 4.64
    row_place = jnp.arange(height, dtype=jnp.float32)[None, None, :, None] / height
    layer_place = jnp.arange(layers, dtype=jnp.float32)[:, None, None, None] / max(layers - 1, 1)
    rising = jnp.exp(0.55 * row_place + 0.55 * layer_place)
    return base * head_scale * row_scale * column_scale * rising


def draw_output_grad(key, part):
    key = jax.random.fold_in(key, 5)
    keys = jax.random.split(key, 3)
    dims = (LAYERS, HEADS, HEAD_DIM, D)
    base = jax.random.normal(keys[0], dims, jnp.float32)
    return shape_grad(keys[2], base).astype(jnp.bfloat16)


def draw_values_grad(key, part):
    key = jax.random.fold_in(key, 7)
    keys = jax.random.split(key, 3)
    dims = (LAYERS, HEADS, KV_OUT, KV_RANK)
    base = jax.random.normal(keys[0], dims, jnp.float32)
    return shape_grad(keys[2], base).astype(jnp.bfloat16)


def level_of(rng, shape, shards, low, largest):
    gain = 1.0
    for axis_at, blocks in shards:
        steps = jax.random.uniform(jax.random.fold_in(jax.random.fold_in(rng, 6), axis_at), (blocks,), jnp.float32, low / len(shards), largest / len(shards))
        gain = gain * jnp.repeat(jnp.exp(steps), shape[axis_at] // blocks).reshape((-1,) + (1,) * (len(shape) - 1 - axis_at))
    return gain


def shared_out(own_key, own, number, rows, amount, top, bound, slope):
    order = jax.random.permutation(own_key, amount)
    crowded, usual = load_shares(amount, rows * top, bound, slope, True), load_shares(amount, rows * top, bound, slope, False)
    places = jnp.arange(amount)

    def named(lengths, rotation):
        used = int((lengths > 0).sum())
        fixed = max(1, used // 4)
        moved = fixed + (places - fixed + rotation * (used - fixed)) % max(1, amount - fixed)
        return jnp.zeros((amount,), jnp.int32).at[order[jnp.where(places < fixed, places, moved)]].set(jnp.asarray(lengths, jnp.int32))

    lengths = jnp.where(number % 4 == 0, named(crowded, number // 4), named(usual, number - number // 4 - 1))
    mixed = jax.random.permutation(jax.random.fold_in(own, 3), amount)
    source_of, receiver = mixed[0:amount // 2 * 2:2], mixed[1:amount // 2 * 2:2]
    slack = jnp.minimum(lengths[source_of] - 1, bound - lengths[receiver]) // 2
    slack = jnp.where((source_of == order[0]) | (receiver == order[0]) | (lengths[receiver] == 0), 0, jnp.maximum(slack, 0))
    moved = jax.random.randint(jax.random.fold_in(own, 4), (amount // 2,), 0, 1 << 20) % (slack + 1)
    lengths = lengths.at[source_of].add(-moved).at[receiver].add(moved)
    items = jnp.searchsorted(jnp.cumsum(lengths), jnp.arange(rows * top), side="right").astype(jnp.int32)
    table = items.reshape(top, rows).T
    table = table[jax.random.permutation(jax.random.fold_in(own, 1), rows)]
    rotation = jax.random.randint(jax.random.fold_in(own, 2), (rows, 1), 0, top)
    return jnp.take_along_axis(table, (jnp.arange(top)[None, :] + rotation) % top, axis=1)


def load_shares(amount, total, limit, slope, full):
    portions = [(1 << 20) // math.isqrt(standing ** slope) + 1 for standing in range(1, amount + 1)]
    largest = limit if full else min(limit, max(-(-total // amount), total * portions[0] // sum(portions)))
    least = 1 if total - largest >= amount - 1 else 0
    holding, rest = [largest] + [least] * (amount - 1), total - largest - least * (amount - 1)
    while rest > 0:
        candidates = [i for i in range(1, amount) if holding[i] < largest] or [i for i in range(1, amount) if holding[i] < limit]
        whole, remaining = sum([portions[i] for i in candidates]), rest
        for i in candidates:
            addition = min(limit - holding[i], max(1, remaining * portions[i] // whole), rest)
            holding[i] = holding[i] + addition
            rest = rest - addition
    return np.array(holding)


def centred(own_key, shape, scale, most, shards=(), held_as=jnp.bfloat16):
    loudness = level_of(own_key, shape, shards, -0.22, 0.18) if shards else 1.0
    result = jax.random.normal(own_key, shape, jnp.float32) * scale * loudness
    return jnp.minimum(jnp.maximum(result, -most), most).astype(held_as)


def setup_inputs(seed: int = 0) -> dict:
    splits = jax.random.split(jax.random.key(seed), 6)
    output_grad = draw_output_grad(jax.random.fold_in(splits[5], 71), 0)
    output_momentum = centred(splits[1], (LAYERS, HEADS, HEAD_DIM, D), 0.5, 3.0, ((0, 4), (2, 64)), jnp.float32)
    values_grad = draw_values_grad(jax.random.fold_in(splits[5], 71), 0)
    values_momentum = centred(splits[3], (LAYERS, HEADS, KV_OUT, KV_RANK), 0.5, 3.0, ((0, 4), (2, 64)), jnp.float32)
    owner_table_keys = jax.random.split(jax.random.fold_in(splits[4], 1), LAYERS * 2 * HEADS // HEADS)
    owner_table_turns = jax.random.permutation(jax.random.fold_in(splits[4], 3), LAYERS * 2 * HEADS // HEADS)
    owner_table = jax.vmap(lambda own, number: shared_out(jax.random.fold_in(splits[4], 2), own, number, HEADS, OWNERS, 1, CAP, 2))(owner_table_keys, owner_table_turns).reshape((LAYERS, 2, HEADS, 1))
    return {"output_grad": output_grad, "output_momentum": output_momentum, "values_grad": values_grad, "values_momentum": values_momentum, "owner_table": owner_table}


MOMENT = 0.95
COEF_A = 3.4445
COEF_B = -4.775
COEF_C = 2.0315
CLIP_RMS = 0.5

def orthogonalize(blocks):
    height, breadth = (blocks.shape[1], blocks.shape[2])
    widened = blocks.astype(jnp.float32)
    squares = lax.optimization_barrier(jnp.sum(widened * widened, axis=(1, 2)))
    current = (widened / (jnp.sqrt(squares) + 1e-07)[:, None, None]).astype(jnp.bfloat16)
    for iteration in range(ITERS):
        gram_matrix = jnp.einsum('krc,ksc->krs', current.astype(jnp.float32), current.astype(jnp.float32)).astype(jnp.bfloat16)
        squared = jnp.einsum('krs,kst->krt', gram_matrix.astype(jnp.float32), gram_matrix.astype(jnp.float32))
        polynomial = (COEF_B * gram_matrix.astype(jnp.float32) + COEF_C * squared).astype(jnp.bfloat16)
        product = jnp.einsum('krs,ksc->krc', polynomial.astype(jnp.float32), current.astype(jnp.float32))
        current = (COEF_A * current.astype(jnp.float32) + product).astype(jnp.bfloat16)
    update = (math.sqrt(max(height, breadth)) * current.astype(jnp.float32)).astype(jnp.bfloat16)
    spread = jnp.sqrt(squares / (height * breadth))
    return (update, spread)

def slot_values(owners_row, spread):
    count = owners_row.shape[0]
    heads_index = jnp.arange(count, dtype=jnp.int32)
    same_owner = owners_row[:, None] == owners_row[None, :]
    earlier = heads_index[None, :] < heads_index[:, None]
    ranks = lax.optimization_barrier(jnp.sum((same_owner & earlier).astype(jnp.int32), axis=1)).astype(jnp.int32)
    flat_slot = (owners_row * CAP + ranks).astype(jnp.int32)
    table_slots = jnp.zeros((OWNERS * CAP,), spread.dtype).at[flat_slot].set(spread)
    return table_slots.reshape(OWNERS, CAP)

def reference(output_grad, output_momentum, values_grad, values_momentum, owner_table):
    out_wide = output_grad.astype(jnp.float32)
    val_wide = values_grad.astype(jnp.float32)
    total = jnp.sum(out_wide * out_wide) + jnp.sum(val_wide * val_wide)
    element_count = LAYERS * HEADS * (HEAD_DIM * D + KV_OUT * KV_RANK)
    clip_factor = jnp.minimum(1.0, CLIP_RMS * math.sqrt(element_count) / jnp.sqrt(total + 1e-06))
    output_next = MOMENT * output_momentum + clip_factor * out_wide
    values_next = MOMENT * values_momentum + clip_factor * val_wide
    out_send = (clip_factor * out_wide + MOMENT * output_next).astype(jnp.bfloat16)
    val_send = (clip_factor * val_wide + MOMENT * values_next).astype(jnp.bfloat16)
    out_updates = []
    val_updates = []
    layer_slots = []
    for layer in range(LAYERS):
        out_update, out_spread = orthogonalize(out_send[layer])
        val_update, val_spread = orthogonalize(val_send[layer])
        out_updates.append(out_update)
        val_updates.append(val_update)
        first = slot_values(owner_table[layer, 0, :, 0], out_spread)
        second = slot_values(owner_table[layer, 1, :, 0], val_spread)
        layer_slots.append(jnp.stack([first, second]))
    return (jnp.stack(out_updates), output_next, jnp.stack(val_updates), values_next, jnp.stack(layer_slots))
```

```python
import functools
import math

import jax
import jax.numpy as jnp
from jax import lax
from jax.experimental import pallas as pl
from jax.experimental.pallas import tpu as pltpu
from jax.sharding import PartitionSpec as P

MOMENT = 0.95
COEF_A = 3.4445
COEF_B = -4.775
COEF_C = 2.0315
CLIP_RMS = 0.5
LANES = 128
F32 = jnp.float32
BF16 = jnp.bfloat16


def flat(x):
    heads, rows, columns = x.shape
    x = x.reshape(heads, rows, columns // LANES, LANES).transpose(0, 2, 1, 3)
    return x.reshape(heads, rows * columns // LANES, LANES)


def unflat(x, rows):
    heads, depth, _ = x.shape
    x = x.reshape(heads, depth // rows, rows, LANES).transpose(0, 2, 1, 3)
    return x.reshape(heads, rows, depth // rows * LANES)


def squares_kernel(out_ref, val_ref, sum_ref):
    total = jnp.zeros((8, LANES), F32)
    for ref in (out_ref, val_ref):
        wide = ref[...].astype(F32).reshape(-1, 8, LANES)
        total = total + jnp.sum(wide * wide, axis=0)
    sum_ref[...] = jnp.broadcast_to(jnp.sum(total, axis=0, keepdims=True), sum_ref.shape)


def local_squares(out_grad, val_grad, pieces):
    vmem = pl.BlockSpec(memory_space=pltpu.VMEM)
    return pl.pallas_call(
        squares_kernel,
        in_specs=[vmem, vmem],
        out_specs=vmem,
        out_shape=jax.ShapeDtypeStruct((pieces, LANES), F32),
        compiler_params=pltpu.CompilerParams(vmem_limit_bytes=16 * 1024 * 1024),
        name="squares",
    )(out_grad, val_grad)


def prepare_kernel(om_ref, vm_ref, decayed_ref):
    depth = om_ref.shape[1]
    decayed_ref[:, :depth, :] = (MOMENT * MOMENT) * om_ref[...]
    decayed_ref[:, depth:, :] = (MOMENT * MOMENT) * vm_ref[...]


def prepare(out_momentum, val_momentum):
    heads = out_momentum.shape[0]
    depth = out_momentum.shape[1] + val_momentum.shape[1]
    vmem = pl.BlockSpec(memory_space=pltpu.VMEM)
    return pl.pallas_call(
        prepare_kernel,
        in_specs=[vmem, vmem],
        out_specs=vmem,
        out_shape=jax.ShapeDtypeStruct((heads, depth, LANES), F32),
        compiler_params=pltpu.CompilerParams(vmem_limit_bytes=16 * 1024 * 1024),
        name="prepare",
    )(out_momentum, val_momentum)


def clip_of(parts, count):
    total = jnp.sum(jnp.sum(parts, axis=0, keepdims=True), axis=1, keepdims=True)
    return jnp.minimum(1.0, CLIP_RMS * math.sqrt(count) / jnp.sqrt(total + 1e-06))


def send_kernel(count, parts_ref, og_ref, vg_ref, decayed_ref, send_ref, clip_ref):
    clip = jnp.broadcast_to(clip_of(parts_ref[...], count), clip_ref.shape)
    clip_ref[...] = clip
    factor = ((1.0 + MOMENT) * clip[0:1]).reshape(1, 1, LANES)
    depth = og_ref.shape[1]
    send_ref[:, :depth, :] = (factor * og_ref[...].astype(F32) + decayed_ref[:, :depth, :]).astype(BF16)
    send_ref[:, depth:, :] = (factor * vg_ref[...].astype(F32) + decayed_ref[:, depth:, :]).astype(BF16)


def rows_to_send(parts, count, out_grad, val_grad, decayed):
    vmem = pl.BlockSpec(memory_space=pltpu.VMEM)
    return pl.pallas_call(
        functools.partial(send_kernel, count),
        in_specs=[vmem] * 4,
        out_specs=[vmem, vmem],
        out_shape=[jax.ShapeDtypeStruct(decayed.shape, BF16), jax.ShapeDtypeStruct((8, LANES), F32)],
        compiler_params=pltpu.CompilerParams(vmem_limit_bytes=24 * 1024 * 1024),
        name="send",
    )(parts, out_grad, val_grad, decayed)


def next_kernel(clip_ref, og_ref, om_ref, vg_ref, vm_ref, on_ref, vn_ref):
    clip = clip_ref[0:1, :].reshape(1, 1, LANES)
    on_ref[...] = MOMENT * om_ref[...] + clip * og_ref[...].astype(F32)
    vn_ref[...] = MOMENT * vm_ref[...] + clip * vg_ref[...].astype(F32)


def next_momentum(clip, out_grad, out_momentum, val_grad, val_momentum, steps=8):
    heads = out_grad.shape[0]
    block = heads // steps

    def spec(x):
        return pl.BlockSpec((block,) + x.shape[1:], lambda i: (i, 0, 0))

    return pl.pallas_call(
        next_kernel,
        grid=(steps,),
        in_specs=[pl.BlockSpec((8, LANES), lambda i: (0, 0))]
        + [spec(x) for x in (out_grad, out_momentum, val_grad, val_momentum)],
        out_specs=[spec(out_grad), spec(val_grad)],
        out_shape=[jax.ShapeDtypeStruct(x.shape, F32) for x in (out_grad, val_grad)],
        name="next",
    )(clip, out_grad, out_momentum, val_grad, val_momentum)


def dot(a, b):
    return lax.dot_general(a.astype(BF16), b.astype(BF16), (((1,), (0,)), ((), ())), preferred_element_type=F32)


def polynomial(gram):
    size = gram.shape[0]
    rows = lax.broadcasted_iota(jnp.int32, gram.shape, 0)
    columns = lax.broadcasted_iota(jnp.int32, gram.shape, 1)
    diagonal = jnp.where(rows == columns, gram, 0.0)
    squares = jnp.sum(jnp.sum(diagonal, axis=0, keepdims=True), axis=1, keepdims=True)
    scale = 1.0 / (jnp.sqrt(squares) + 1e-07)
    gram = (gram * scale) * scale
    first = COEF_B * gram + COEF_C * dot(gram, gram)
    bent = dot(first, gram)
    gram = COEF_A * COEF_A * gram + 2.0 * COEF_A * bent + dot(first, bent)
    second = COEF_B * gram + COEF_C * dot(gram, gram)
    return squares, scale, COEF_A * (first + second) + dot(second, first)


def thirds(value):
    high = value.astype(BF16).astype(F32)
    middle = (value - high).astype(BF16).astype(F32)
    low = value - high - middle
    lane = lax.broadcasted_iota(jnp.int32, (1, LANES), 1)
    return jnp.where(lane == 0, high, jnp.where(lane == 1, middle, jnp.where(lane == 2, low, 0.0)))


def orthogonal_kernel(sizes, got_ref, back_ref, wide_ref, out_ref, val_ref):
    (out_rows, out_columns), (val_rows, val_columns) = sizes
    sources = out_ref.shape[0] // out_rows
    taken, given = got_ref.shape[0] // sources, back_ref.shape[0] // sources
    pitch = wide_ref.shape[0] // sources

    def spread_out(s, _):
        wide_ref[pl.ds(pl.multiple_of(s * pitch, 8), taken), :] = got_ref[
            pl.ds(pl.multiple_of(s * taken, 16), taken), :
        ].astype(F32)
        return 0

    lax.fori_loop(0, sources, spread_out, 0, unroll=4)

    offset = 0
    for ref, rows, columns in ((out_ref, out_rows, out_columns), (val_ref, val_rows, val_columns)):
        for j in range(columns // LANES):
            parts = [
                wide_ref[pl.ds(offset + j * rows + r, sources, stride=pitch), :].astype(BF16) for r in range(rows)
            ]
            ref[:, j * LANES : (j + 1) * LANES] = jnp.concatenate(parts, axis=0)
        offset += columns // LANES * rows

    offset = 0
    spreads = []
    for ref, rows, columns in ((out_ref, out_rows, out_columns), (val_ref, val_rows, val_columns)):
        whole = ref[...]
        gram = lax.dot_general(whole, whole, (((1,), (1,)), ((), ())), preferred_element_type=F32)
        squares, scale, factor = polynomial(gram)
        factor = factor.astype(BF16)
        height = rows * sources
        final = scale * math.sqrt(max(height, columns))
        spreads.append(jnp.sqrt(squares / (height * columns)))
        width = 512
        for at in range(columns // width):
            piece = ref[:, at * width : (at + 1) * width]
            product = lax.dot_general(factor, piece, (((1,), (0,)), ((), ())), preferred_element_type=F32)
            product = final * (COEF_A * COEF_A * piece.astype(F32) + product)
            for k in range(width // LANES):
                j = at * (width // LANES) + k
                for r in range(rows):
                    wide_ref[pl.ds(offset + j * rows + r, sources, stride=given), :] = product[
                        r * sources : (r + 1) * sources, k * LANES : (k + 1) * LANES
                    ]
        offset += columns // LANES * rows
    for r, spread in enumerate(spreads):
        wide_ref[pl.ds(offset + r, sources, stride=given), :] = jnp.broadcast_to(thirds(spread), (sources, LANES))

    chunk = given * 8

    def gather(i, _):
        rows = pl.ds(pl.multiple_of(i * chunk, 16), chunk)
        back_ref[rows, :] = wide_ref[rows, :].astype(BF16)
        return 0

    lax.fori_loop(0, sources // 8, gather, 0)


def orthogonalize(got, sizes, sources, given, pitch=136):
    (out_rows, out_columns), (val_rows, val_columns) = sizes
    return pl.pallas_call(
        functools.partial(orthogonal_kernel, sizes),
        out_shape=jax.ShapeDtypeStruct((sources * given, LANES), BF16),
        scratch_shapes=[
            pltpu.VMEM((sources * pitch, LANES), F32),
            pltpu.VMEM((out_rows * sources, out_columns), BF16),
            pltpu.VMEM((val_rows * sources, val_columns), BF16),
        ],
        compiler_params=pltpu.CompilerParams(vmem_limit_bytes=40 * 1024 * 1024),
        name="orthogonal",
    )(got)


def finish_kernel(given, back_ref, choice_ref, out_ref, val_ref, slot_ref):
    @pl.when(pl.program_id(0) == 0)
    def _():
        slot_ref[...] = jnp.zeros_like(slot_ref)

    block, out_depth, _ = out_ref.shape
    val_depth = val_ref.shape[1]
    total = jnp.zeros(slot_ref.shape, F32)
    for p in range(block):
        start = p * given
        out_ref[p] = back_ref[start : start + out_depth, :]
        start += out_depth
        val_ref[p] = back_ref[start : start + val_depth, :]
        start += val_depth
        spread = jnp.sum(back_ref[start : start + 2, :].astype(F32), axis=1, keepdims=True)
        total = total + spread * choice_ref[p]
    slot_ref[...] += total


def finish(back, choice, out_depth, val_depth, given, steps=8):
    heads = choice.shape[0]
    block = heads // steps

    def spec(depth):
        return pl.BlockSpec((block, depth, LANES), lambda i: (i, 0, 0))

    return pl.pallas_call(
        functools.partial(finish_kernel, given),
        grid=(steps,),
        in_specs=[pl.BlockSpec((block * given, LANES), lambda i: (i, 0)), spec(2)],
        out_specs=[spec(out_depth), spec(val_depth), pl.BlockSpec((2, LANES), lambda i: (0, 0))],
        out_shape=[
            jax.ShapeDtypeStruct((heads, out_depth, LANES), BF16),
            jax.ShapeDtypeStruct((heads, val_depth, LANES), BF16),
            jax.ShapeDtypeStruct((2, LANES), F32),
        ],
        name="finish",
    )(back, choice)


def slot_choice(table, owner):
    mine = (table == owner).astype(jnp.int32)
    heads = mine.shape[1]
    index = lax.iota(jnp.int32, heads)
    earlier = (index[None, :] < index[:, None]).astype(jnp.int32)
    rank = jnp.sum(earlier[None] * mine[:, None, :], axis=2)
    lane = lax.iota(jnp.int32, LANES)
    chosen = (mine[:, :, None] == 1) & (rank[:, :, None] == lane[None, None, :])
    return chosen.astype(F32).transpose(1, 0, 2)


def body(output_grad, output_momentum, values_grad, values_momentum, owner_table):
    owners, layers = lax.axis_size("dp"), lax.axis_size("layer")
    out_rows, out_columns = output_grad.shape[2:]
    val_rows, val_columns = values_grad.shape[2:]
    capacity = 3
    out_grad, out_momentum = flat(output_grad[0]), flat(output_momentum[0])
    val_grad, val_momentum = flat(values_grad[0]), flat(values_momentum[0])
    heads = out_grad.shape[0]

    everyone = owners * layers
    parts = lax.all_to_all(
        local_squares(out_grad, val_grad, everyone).reshape(everyone, 1, LANES),
        ("dp", "layer"),
        split_axis=0,
        concat_axis=0,
        tiled=True,
    ).reshape(everyone, LANES)
    count = (output_grad.size + values_grad.size) * everyone

    decayed = prepare(out_momentum, val_momentum)
    send, clip = rows_to_send(parts, count, out_grad, val_grad, decayed)
    out_next, val_next = next_momentum(clip, out_grad, out_momentum, val_grad, val_momentum)
    got = lax.all_to_all(send, "dp", split_axis=0, concat_axis=0, tiled=True)

    out_depth, val_depth = out_grad.shape[1], val_grad.shape[1]
    given = out_depth + val_depth + 2
    back = orthogonalize(
        got.reshape(heads * (out_depth + val_depth), LANES),
        ((out_rows, out_columns), (val_rows, val_columns)),
        owners,
        given,
    )
    back = lax.all_to_all(
        back.reshape(heads, given // 2, 2, LANES), "dp", split_axis=0, concat_axis=0, tiled=True
    )
    choice = slot_choice(owner_table[0, :, :, 0], lax.axis_index("dp"))
    out_update, val_update, slots = finish(
        back.reshape(heads * given, LANES), choice, out_depth, val_depth, given
    )

    return (
        unflat(out_update.reshape(out_grad.shape), out_rows)[None],
        unflat(out_next, out_rows)[None],
        unflat(val_update.reshape(val_grad.shape), val_rows)[None],
        unflat(val_next, val_rows)[None],
        slots[None, :, None, :capacity],
    )


def solution(mesh):
    rows = P("layer", None, "dp", None)
    return jax.shard_map(
        body,
        mesh=mesh,
        in_specs=(rows, rows, rows, rows, P("layer", None, None, None)),
        out_specs=(rows, rows, rows, rows, rows),
        check_vma=False,
    )
```

```python
import functools
import math

import jax
import jax.numpy as jnp
from jax import lax
from jax.experimental import pallas as pl
from jax.experimental.pallas import tpu as pltpu
from jax.sharding import PartitionSpec as P

MOMENT = 0.95
COEF_A = 3.4445
COEF_B = -4.775
COEF_C = 2.0315
CLIP_RMS = 0.5
LANES = 128
F32 = jnp.float32
BF16 = jnp.bfloat16


def flat(x):
    heads, rows, columns = x.shape
    x = x.reshape(heads, rows, columns // LANES, LANES).transpose(0, 2, 1, 3)
    return x.reshape(heads, rows * columns // LANES, LANES)


def unflat(x, rows):
    heads, depth, _ = x.shape
    x = x.reshape(heads, depth // rows, rows, LANES).transpose(0, 2, 1, 3)
    return x.reshape(heads, rows, depth // rows * LANES)


HBM = pl.BlockSpec(memory_space=pltpu.HBM)
VMEM = pl.BlockSpec(memory_space=pltpu.VMEM)
CHUNKS = 8
GRANT = 60 * 1024 * 1024
ORTHO = 40 * 1024 * 1024


def chunk_of(ref, i):
    block = ref.shape[0] // CHUNKS
    return ref.at[pl.ds(i * block, block)]


def loads(pairs, sems):
    copies = []
    for i in range(CHUNKS):
        row = []
        for n, (source, target) in enumerate(pairs):
            copy = pltpu.make_async_copy(chunk_of(source, i), chunk_of(target, i), sems.at[n, i])
            copy.start()
            row.append(copy)
        copies.append(row)
    return copies


def squares_kernel(out_hbm, val_hbm, sum_ref, out_ref, val_ref, sems):
    copies = loads([(out_hbm, out_ref), (val_hbm, val_ref)], sems)
    total = jnp.zeros((8, LANES), F32)
    for i, row in enumerate(copies):
        for copy, ref in zip(row, (out_ref, val_ref)):
            copy.wait()
            wide = chunk_of(ref, i)[...].astype(F32).reshape(-1, 8, LANES)
            total = total + jnp.sum(wide * wide, axis=0)
    sum_ref[...] = jnp.broadcast_to(jnp.sum(total, axis=0, keepdims=True), sum_ref.shape)


def local_squares(out_grad, val_grad, pieces):
    return pl.pallas_call(
        squares_kernel,
        in_specs=[HBM, HBM],
        out_specs=VMEM,
        out_shape=jax.ShapeDtypeStruct((pieces, LANES), F32),
        scratch_shapes=[
            pltpu.VMEM(out_grad.shape, BF16),
            pltpu.VMEM(val_grad.shape, BF16),
            pltpu.SemaphoreType.DMA((2, CHUNKS)),
        ],
        compiler_params=pltpu.CompilerParams(vmem_limit_bytes=GRANT),
        name="squares",
    )(out_grad, val_grad)


def prepare_kernel(om_ref, vm_ref, decayed_ref):
    depth = om_ref.shape[1]
    decayed_ref[:, :depth, :] = (MOMENT * MOMENT) * om_ref[...]
    decayed_ref[:, depth:, :] = (MOMENT * MOMENT) * vm_ref[...]


def prepare(out_momentum, val_momentum):
    heads = out_momentum.shape[0]
    depth = out_momentum.shape[1] + val_momentum.shape[1]
    return pl.pallas_call(
        prepare_kernel,
        in_specs=[VMEM, VMEM],
        out_specs=VMEM,
        out_shape=jax.ShapeDtypeStruct((heads, depth, LANES), F32),
        compiler_params=pltpu.CompilerParams(vmem_limit_bytes=16 * 1024 * 1024),
        name="prepare",
    )(out_momentum, val_momentum)


def clip_of(parts, count):
    total = jnp.sum(jnp.sum(parts, axis=0, keepdims=True), axis=1, keepdims=True)
    return jnp.minimum(1.0, CLIP_RMS * math.sqrt(count) / jnp.sqrt(total + 1e-06))


def send_kernel(count, parts_ref, og_ref, vg_ref, decayed_ref, send_ref, clip_ref):
    clip = jnp.broadcast_to(clip_of(parts_ref[...], count), clip_ref.shape)
    clip_ref[...] = clip
    factor = ((1.0 + MOMENT) * clip[0:1]).reshape(1, 1, LANES)
    depth = og_ref.shape[1]
    send_ref[:, :depth, :] = (factor * og_ref[...].astype(F32) + decayed_ref[:, :depth, :]).astype(BF16)
    send_ref[:, depth:, :] = (factor * vg_ref[...].astype(F32) + decayed_ref[:, depth:, :]).astype(BF16)


def rows_to_send(parts, count, out_grad, val_grad, decayed):
    return pl.pallas_call(
        functools.partial(send_kernel, count),
        in_specs=[VMEM] * 4,
        out_specs=[VMEM, VMEM],
        out_shape=[jax.ShapeDtypeStruct(decayed.shape, BF16), jax.ShapeDtypeStruct((8, LANES), F32)],
        compiler_params=pltpu.CompilerParams(vmem_limit_bytes=24 * 1024 * 1024),
        name="send",
    )(parts, out_grad, val_grad, decayed)


def next_kernel(clip_ref, og_ref, om_ref, vg_ref, vm_ref, on_ref, vn_ref):
    clip = clip_ref[0:1, :].reshape(1, 1, LANES)
    on_ref[...] = MOMENT * om_ref[...] + clip * og_ref[...].astype(F32)
    vn_ref[...] = MOMENT * vm_ref[...] + clip * vg_ref[...].astype(F32)


def next_momentum(clip, out_grad, out_momentum, val_grad, val_momentum, steps=8):
    heads = out_grad.shape[0]
    block = heads // steps

    def spec(x):
        return pl.BlockSpec((block,) + x.shape[1:], lambda i: (i, 0, 0))

    return pl.pallas_call(
        next_kernel,
        grid=(steps,),
        in_specs=[pl.BlockSpec((8, LANES), lambda i: (0, 0))]
        + [spec(x) for x in (out_grad, out_momentum, val_grad, val_momentum)],
        out_specs=[spec(out_grad), spec(val_grad)],
        out_shape=[jax.ShapeDtypeStruct(x.shape, F32) for x in (out_grad, val_grad)],
        name="next",
    )(clip, out_grad, out_momentum, val_grad, val_momentum)


def dot(a, b):
    return lax.dot_general(a.astype(BF16), b.astype(BF16), (((1,), (0,)), ((), ())), preferred_element_type=F32)


def polynomials(grams):
    every, scales = [], []
    for gram in grams:
        rows = lax.broadcasted_iota(jnp.int32, gram.shape, 0)
        columns = lax.broadcasted_iota(jnp.int32, gram.shape, 1)
        diagonal = jnp.where(rows == columns, gram, 0.0)
        squares = jnp.sum(jnp.sum(diagonal, axis=0, keepdims=True), axis=1, keepdims=True)
        every.append(squares)
        scales.append(1.0 / (jnp.sqrt(squares) + 1e-07))
    grams = [(gram * scale) * scale for gram, scale in zip(grams, scales)]
    first = [COEF_B * gram + COEF_C * dot(gram, gram) for gram in grams]
    bent = [dot(f, gram) for f, gram in zip(first, grams)]
    grams = [
        COEF_A * COEF_A * gram + 2.0 * COEF_A * b + dot(f, b) for f, gram, b in zip(first, grams, bent)
    ]
    second = [COEF_B * gram + COEF_C * dot(gram, gram) for gram in grams]
    return every, scales, [COEF_A * (f + g) + dot(g, f) for f, g in zip(first, second)]


def thirds(value):
    high = value.astype(BF16).astype(F32)
    middle = (value - high).astype(BF16).astype(F32)
    low = value - high - middle
    lane = lax.broadcasted_iota(jnp.int32, (1, LANES), 1)
    return jnp.where(lane == 0, high, jnp.where(lane == 1, middle, jnp.where(lane == 2, low, 0.0)))


def orthogonal_kernel(sizes, got_ref, back_hbm, wide_ref, back_ref, out_ref, val_ref, sems):
    sources, depth, _ = got_ref.shape
    pitch, given = wide_ref.shape[0] // sources, back_ref.shape[0] // sources
    matrices = [(ref, rows, columns) for ref, (rows, columns) in zip((out_ref, val_ref), sizes)]
    for s in range(sources):
        wide_ref[s * pitch : s * pitch + depth, :] = got_ref[s].astype(F32)

    offset = 0
    grams = []
    for ref, rows, columns in matrices:
        for j in range(columns // LANES):
            parts = [
                wide_ref[pl.ds(offset + j * rows + r, sources, stride=pitch), :].astype(BF16) for r in range(rows)
            ]
            ref[:, j * LANES : (j + 1) * LANES] = jnp.concatenate(parts, axis=0)
        offset += columns // LANES * rows
        whole = ref[...]
        grams.append(lax.dot_general(whole, whole, (((1,), (1,)), ((), ())), preferred_element_type=F32))
    squares, scales, factors = polynomials(grams)

    offset = 0
    for (ref, rows, columns), scale, factor in zip(matrices, scales, factors):
        factor = factor.astype(BF16)
        final = scale * math.sqrt(max(rows * sources, columns))
        width = 512
        for at in range(0, columns, width):
            piece = ref[:, at : at + width]
            product = lax.dot_general(factor, piece, (((1,), (0,)), ((), ())), preferred_element_type=F32)
            product = final * (COEF_A * COEF_A * piece.astype(F32) + product)
            for k in range(width // LANES):
                j = at // LANES + k
                for r in range(rows):
                    wide_ref[pl.ds(offset + j * rows + r, sources, stride=given), :] = product[
                        r * sources : (r + 1) * sources, k * LANES : (k + 1) * LANES
                    ]
        offset += columns // LANES * rows

    for r, ((_, rows, columns), square) in enumerate(zip(matrices, squares)):
        spread = jnp.sqrt(square / (rows * sources * columns))
        wide_ref[pl.ds(offset + r, sources, stride=given), :] = jnp.broadcast_to(thirds(spread), (sources, LANES))

    copies = []
    for i in range(CHUNKS):
        block = back_ref.shape[0] // CHUNKS
        back_ref[i * block : (i + 1) * block, :] = wide_ref[i * block : (i + 1) * block, :].astype(BF16)
        copy = pltpu.make_async_copy(chunk_of(back_ref, i), chunk_of(back_hbm, i), sems.at[i])
        copy.start()
        copies.append(copy)
    for copy in copies:
        copy.wait()


def orthogonalize(got, sizes, given, pitch=136):
    sources = got.shape[0]
    return pl.pallas_call(
        functools.partial(orthogonal_kernel, sizes),
        in_specs=[VMEM],
        out_specs=HBM,
        out_shape=jax.ShapeDtypeStruct((sources * given, LANES), BF16),
        scratch_shapes=[pltpu.VMEM((sources * pitch, LANES), F32), pltpu.VMEM((sources * given, LANES), BF16)]
        + [pltpu.VMEM((rows * sources, columns), BF16) for rows, columns in sizes]
        + [pltpu.SemaphoreType.DMA((CHUNKS,))],
        compiler_params=pltpu.CompilerParams(vmem_limit_bytes=ORTHO),
        name="orthogonal",
    )(got)


def finish_kernel(given, back_ref, choice_ref, out_hbm, val_hbm, slot_ref, wide_ref, out_ref, val_ref, sems):
    heads, out_depth, _ = out_ref.shape
    val_depth = val_ref.shape[1]
    block = heads // CHUNKS
    total = jnp.zeros(slot_ref.shape, F32)
    copies = []
    for i in range(CHUNKS):
        span = pl.ds(i * block * given, block * given)
        wide_ref[span, :] = back_ref[span, :].astype(F32)
        for p in range(i * block, (i + 1) * block):
            start = p * given
            out_ref[p] = wide_ref[start : start + out_depth, :].astype(BF16)
            start += out_depth
            val_ref[p] = wide_ref[start : start + val_depth, :].astype(BF16)
            start += val_depth
            spread = jnp.sum(wide_ref[start : start + 2, :], axis=1, keepdims=True)
            total = total + spread * choice_ref[p]
        for n, (ref, target) in enumerate(((out_ref, out_hbm), (val_ref, val_hbm))):
            copy = pltpu.make_async_copy(chunk_of(ref, i), chunk_of(target, i), sems.at[n, i])
            copy.start()
            copies.append(copy)
    slot_ref[...] = total
    for copy in copies:
        copy.wait()


def finish(back, choice, out_depth, val_depth, given):
    heads = choice.shape[0]
    shapes = [(heads, rows, LANES) for rows in (out_depth, val_depth)]
    return pl.pallas_call(
        functools.partial(finish_kernel, given),
        in_specs=[VMEM, VMEM],
        out_specs=[HBM, HBM, VMEM],
        out_shape=[jax.ShapeDtypeStruct(shape, BF16) for shape in shapes] + [jax.ShapeDtypeStruct((2, LANES), F32)],
        scratch_shapes=[pltpu.VMEM(back.shape, F32)]
        + [pltpu.VMEM(shape, BF16) for shape in shapes]
        + [pltpu.SemaphoreType.DMA((2, CHUNKS))],
        compiler_params=pltpu.CompilerParams(vmem_limit_bytes=24 * 1024 * 1024),
        name="finish",
    )(back, choice)


def slot_choice(table, owner):
    mine = (table == owner).astype(jnp.int32)
    heads = mine.shape[1]
    index = lax.iota(jnp.int32, heads)
    earlier = (index[None, :] < index[:, None]).astype(jnp.int32)
    rank = jnp.sum(earlier[None] * mine[:, None, :], axis=2)
    lane = lax.iota(jnp.int32, LANES)
    chosen = (mine[:, :, None] == 1) & (rank[:, :, None] == lane[None, None, :])
    return chosen.astype(F32).transpose(1, 0, 2)


def body(output_grad, output_momentum, values_grad, values_momentum, owner_table):
    owners, layers = lax.axis_size("dp"), lax.axis_size("layer")
    out_rows, out_columns = output_grad.shape[2:]
    val_rows, val_columns = values_grad.shape[2:]
    capacity = 3
    out_grad, out_momentum = flat(output_grad[0]), flat(output_momentum[0])
    val_grad, val_momentum = flat(values_grad[0]), flat(values_momentum[0])
    heads = out_grad.shape[0]

    everyone = owners * layers
    parts = lax.all_to_all(
        local_squares(out_grad, val_grad, everyone).reshape(everyone, 1, LANES),
        ("dp", "layer"),
        split_axis=0,
        concat_axis=0,
        tiled=True,
    ).reshape(everyone, LANES)
    count = (output_grad.size + values_grad.size) * everyone

    decayed = prepare(out_momentum, val_momentum)
    send, clip = rows_to_send(parts, count, out_grad, val_grad, decayed)
    out_next, val_next = next_momentum(clip, out_grad, out_momentum, val_grad, val_momentum)
    got = lax.all_to_all(send, "dp", split_axis=0, concat_axis=0, tiled=True)

    out_depth, val_depth = out_grad.shape[1], val_grad.shape[1]
    given = out_depth + val_depth + 2
    back = orthogonalize(got, ((out_rows, out_columns), (val_rows, val_columns)), given)
    back = lax.all_to_all(
        back.reshape(heads, given // 2, 2, LANES), "dp", split_axis=0, concat_axis=0, tiled=True
    )
    choice = slot_choice(owner_table[0, :, :, 0], lax.axis_index("dp"))
    out_update, val_update, slots = finish(
        back.reshape(heads * given, LANES), choice, out_depth, val_depth, given
    )

    return (
        unflat(out_update.reshape(out_grad.shape), out_rows)[None],
        unflat(out_next, out_rows)[None],
        unflat(val_update.reshape(val_grad.shape), val_rows)[None],
        unflat(val_next, val_rows)[None],
        slots[None, :, None, :capacity],
    )


def solution(mesh):
    rows = P("layer", None, "dp", None)
    return jax.shard_map(
        body,
        mesh=mesh,
        in_specs=(rows, rows, rows, rows, P("layer", None, None, None)),
        out_specs=(rows, rows, rows, rows, rows),
        check_vma=False,
    )
```

```python
import functools
import math

import jax
import jax.numpy as jnp
from jax import lax
from jax.experimental import pallas as pl
from jax.experimental.pallas import tpu as pltpu
from jax.sharding import PartitionSpec as P

MOMENT = 0.95
COEF_A = 3.4445
COEF_B = -4.775
COEF_C = 2.0315
CLIP_RMS = 0.5
LANES = 128
F32 = jnp.float32
BF16 = jnp.bfloat16


def flat(x):
    heads, rows, columns = x.shape
    x = x.reshape(heads, rows, columns // LANES, LANES).transpose(0, 2, 1, 3)
    return x.reshape(heads, rows * columns // LANES, LANES)


def unflat(x, rows):
    heads, depth, _ = x.shape
    x = x.reshape(heads, depth // rows, rows, LANES).transpose(0, 2, 1, 3)
    return x.reshape(heads, rows, depth // rows * LANES)


HBM = pl.BlockSpec(memory_space=pltpu.HBM)
VMEM = pl.BlockSpec(memory_space=pltpu.VMEM)
CHUNKS = 8
GRANT = 60 * 1024 * 1024
ORTHO = 40 * 1024 * 1024


def chunk_of(ref, i):
    block = ref.shape[0] // CHUNKS
    return ref.at[pl.ds(i * block, block)]


def loads(pairs, sems):
    copies = []
    for i in range(CHUNKS):
        row = []
        for n, (source, target) in enumerate(pairs):
            copy = pltpu.make_async_copy(chunk_of(source, i), chunk_of(target, i), sems.at[n, i])
            copy.start()
            row.append(copy)
        copies.append(row)
    return copies


def squares_kernel(out_hbm, val_hbm, sum_ref, out_ref, val_ref, sems):
    copies = loads([(out_hbm, out_ref), (val_hbm, val_ref)], sems)
    total = jnp.zeros((8, LANES), F32)
    for i, row in enumerate(copies):
        for copy, ref in zip(row, (out_ref, val_ref)):
            copy.wait()
            wide = chunk_of(ref, i)[...].astype(F32).reshape(-1, 8, LANES)
            total = total + jnp.sum(wide * wide, axis=0)
    sum_ref[...] = jnp.broadcast_to(jnp.sum(total, axis=0, keepdims=True), sum_ref.shape)


def local_squares(out_grad, val_grad, pieces):
    return pl.pallas_call(
        squares_kernel,
        in_specs=[HBM, HBM],
        out_specs=VMEM,
        out_shape=jax.ShapeDtypeStruct((pieces, LANES), F32),
        scratch_shapes=[
            pltpu.VMEM(out_grad.shape, BF16),
            pltpu.VMEM(val_grad.shape, BF16),
            pltpu.SemaphoreType.DMA((2, CHUNKS)),
        ],
        compiler_params=pltpu.CompilerParams(vmem_limit_bytes=16 * 1024 * 1024),
        name="squares",
    )(*(pltpu.with_memory_space_constraint(x, pltpu.HBM) for x in (out_grad, val_grad)))


def prepare_kernel(om_ref, vm_ref, decayed_ref):
    depth = om_ref.shape[1]
    decayed_ref[:, :depth, :] = (MOMENT * MOMENT) * om_ref[...]
    decayed_ref[:, depth:, :] = (MOMENT * MOMENT) * vm_ref[...]


def prepare(out_momentum, val_momentum):
    heads = out_momentum.shape[0]
    depth = out_momentum.shape[1] + val_momentum.shape[1]
    return pl.pallas_call(
        prepare_kernel,
        in_specs=[VMEM, VMEM],
        out_specs=VMEM,
        out_shape=jax.ShapeDtypeStruct((heads, depth, LANES), F32),
        compiler_params=pltpu.CompilerParams(vmem_limit_bytes=16 * 1024 * 1024),
        name="prepare",
    )(out_momentum, val_momentum)


def row_sum_kernel(parts_ref, sum_ref):
    sum_ref[...] = jnp.broadcast_to(jnp.sum(parts_ref[...], axis=0, keepdims=True), sum_ref.shape)


def row_sum(parts):
    return pl.pallas_call(
        row_sum_kernel,
        in_specs=[VMEM],
        out_specs=VMEM,
        out_shape=jax.ShapeDtypeStruct((8, LANES), F32),
        compiler_params=pltpu.CompilerParams(vmem_limit_bytes=4 * 1024 * 1024),
        name="row_sum",
    )(parts)


def clip_of(parts, count):
    total = jnp.sum(jnp.sum(parts, axis=0, keepdims=True), axis=1, keepdims=True)
    return jnp.minimum(1.0, CLIP_RMS * math.sqrt(count) / jnp.sqrt(total + 1e-06))


def send_kernel(count, layers, *refs):
    parts_refs, refs = refs[:layers], refs[layers:]
    og_ref, vg_ref, decayed_ref, send_ref, clip_hbm, clip_ref, clip_sem = refs
    parts = jnp.concatenate([ref[0:1, :] for ref in parts_refs], axis=0)
    clip = jnp.broadcast_to(clip_of(parts, count), clip_ref.shape)
    clip_ref[...] = clip
    copy = pltpu.make_async_copy(clip_ref, clip_hbm, clip_sem)
    copy.start()
    factor = ((1.0 + MOMENT) * clip[0:1]).reshape(1, 1, LANES)
    depth = og_ref.shape[1]
    send_ref[:, :depth, :] = (factor * og_ref[...].astype(F32) + decayed_ref[:, :depth, :]).astype(BF16)
    send_ref[:, depth:, :] = (factor * vg_ref[...].astype(F32) + decayed_ref[:, depth:, :]).astype(BF16)
    copy.wait()


def rows_to_send(parts, count, out_grad, val_grad, decayed):
    return pl.pallas_call(
        functools.partial(send_kernel, count, len(parts)),
        in_specs=[VMEM] * (len(parts) + 3),
        out_specs=[VMEM, HBM],
        out_shape=[jax.ShapeDtypeStruct(decayed.shape, BF16), pltpu.HBM((8, LANES), F32)],
        scratch_shapes=[pltpu.VMEM((8, LANES), F32), pltpu.SemaphoreType.DMA(())],
        compiler_params=pltpu.CompilerParams(vmem_limit_bytes=24 * 1024 * 1024),
        name="send",
    )(*parts, out_grad, val_grad, decayed)


def next_kernel(clip_ref, og_ref, om_ref, vg_ref, vm_ref, on_ref, vn_ref):
    clip = clip_ref[0:1, :].reshape(1, 1, LANES)
    on_ref[...] = MOMENT * om_ref[...] + clip * og_ref[...].astype(F32)
    vn_ref[...] = MOMENT * vm_ref[...] + clip * vg_ref[...].astype(F32)


def next_momentum(clip, out_grad, out_momentum, val_grad, val_momentum, steps=8):
    heads = out_grad.shape[0]
    block = heads // steps

    def spec(x):
        return pl.BlockSpec((block,) + x.shape[1:], lambda i: (i, 0, 0))

    return pl.pallas_call(
        next_kernel,
        grid=(steps,),
        in_specs=[pl.BlockSpec((8, LANES), lambda i: (0, 0))]
        + [spec(x) for x in (out_grad, out_momentum, val_grad, val_momentum)],
        out_specs=[spec(out_grad), spec(val_grad)],
        out_shape=[jax.ShapeDtypeStruct(x.shape, F32) for x in (out_grad, val_grad)],
        name="next",
    )(clip, out_grad, out_momentum, val_grad, val_momentum)


def dot(a, b):
    return lax.dot_general(a.astype(BF16), b.astype(BF16), (((1,), (0,)), ((), ())), preferred_element_type=F32)


def polynomials(grams):
    every, scales = [], []
    for gram in grams:
        rows = lax.broadcasted_iota(jnp.int32, gram.shape, 0)
        columns = lax.broadcasted_iota(jnp.int32, gram.shape, 1)
        diagonal = jnp.where(rows == columns, gram, 0.0)
        squares = jnp.sum(jnp.sum(diagonal, axis=0, keepdims=True), axis=1, keepdims=True)
        every.append(squares)
        scales.append(1.0 / (jnp.sqrt(squares) + 1e-07))
    grams = [(gram * scale) * scale for gram, scale in zip(grams, scales)]
    first = [COEF_B * gram + COEF_C * dot(gram, gram) for gram in grams]
    bent = [dot(f, gram) for f, gram in zip(first, grams)]
    grams = [
        COEF_A * COEF_A * gram + 2.0 * COEF_A * b + dot(f, b) for f, gram, b in zip(first, grams, bent)
    ]
    second = [COEF_B * gram + COEF_C * dot(gram, gram) for gram in grams]
    return every, scales, [COEF_A * (f + g) + dot(g, f) for f, g in zip(first, second)]


def thirds(value):
    high = value.astype(BF16).astype(F32)
    middle = (value - high).astype(BF16).astype(F32)
    low = value - high - middle
    lane = lax.broadcasted_iota(jnp.int32, (1, LANES), 1)
    return jnp.where(lane == 0, high, jnp.where(lane == 1, middle, jnp.where(lane == 2, low, 0.0)))


def orthogonal_kernel(sizes, got_ref, back_hbm, wide_ref, back_ref, out_ref, val_ref, sems):
    sources, depth, _ = got_ref.shape
    pitch, given = wide_ref.shape[0] // sources, back_ref.shape[0] // sources
    matrices = [(ref, rows, columns) for ref, (rows, columns) in zip((out_ref, val_ref), sizes)]
    for s in range(sources):
        wide_ref[s * pitch : s * pitch + depth, :] = got_ref[s].astype(F32)

    offset = 0
    grams = []
    for ref, rows, columns in matrices:
        for j in range(columns // LANES):
            parts = [
                wide_ref[pl.ds(offset + j * rows + r, sources, stride=pitch), :].astype(BF16) for r in range(rows)
            ]
            ref[:, j * LANES : (j + 1) * LANES] = jnp.concatenate(parts, axis=0)
        offset += columns // LANES * rows
        whole = ref[...]
        grams.append(lax.dot_general(whole, whole, (((1,), (1,)), ((), ())), preferred_element_type=F32))
    squares, scales, factors = polynomials(grams)

    offset = 0
    for (ref, rows, columns), scale, factor in zip(matrices, scales, factors):
        factor = factor.astype(BF16)
        final = scale * math.sqrt(max(rows * sources, columns))
        width = 512
        for at in range(0, columns, width):
            piece = ref[:, at : at + width]
            product = lax.dot_general(factor, piece, (((1,), (0,)), ((), ())), preferred_element_type=F32)
            product = final * (COEF_A * COEF_A * piece.astype(F32) + product)
            for k in range(width // LANES):
                j = at // LANES + k
                for r in range(rows):
                    wide_ref[pl.ds(offset + j * rows + r, sources, stride=given), :] = product[
                        r * sources : (r + 1) * sources, k * LANES : (k + 1) * LANES
                    ]
        offset += columns // LANES * rows

    for r, ((_, rows, columns), square) in enumerate(zip(matrices, squares)):
        spread = jnp.sqrt(square / (rows * sources * columns))
        wide_ref[pl.ds(offset + r, sources, stride=given), :] = jnp.broadcast_to(thirds(spread), (sources, LANES))

    copies = []
    for i in range(CHUNKS):
        block = back_ref.shape[0] // CHUNKS
        back_ref[i * block : (i + 1) * block, :] = wide_ref[i * block : (i + 1) * block, :].astype(BF16)
        copy = pltpu.make_async_copy(chunk_of(back_ref, i), chunk_of(back_hbm, i), sems.at[i])
        copy.start()
        copies.append(copy)
    for copy in copies:
        copy.wait()


def orthogonalize(got, sizes, given, pitch=136):
    sources = got.shape[0]
    return pl.pallas_call(
        functools.partial(orthogonal_kernel, sizes),
        in_specs=[VMEM],
        out_specs=HBM,
        out_shape=pltpu.HBM((sources * given, LANES), BF16),
        scratch_shapes=[pltpu.VMEM((sources * pitch, LANES), F32), pltpu.VMEM((sources * given, LANES), BF16)]
        + [pltpu.VMEM((rows * sources, columns), BF16) for rows, columns in sizes]
        + [pltpu.SemaphoreType.DMA((CHUNKS,))],
        compiler_params=pltpu.CompilerParams(vmem_limit_bytes=ORTHO),
        name="orthogonal",
    )(got)


def finish_kernel(given, back_ref, choice_ref, out_hbm, val_hbm, slot_ref, wide_ref, out_ref, val_ref, sems):
    heads, out_depth, _ = out_ref.shape
    val_depth = val_ref.shape[1]
    block = heads // CHUNKS
    total = jnp.zeros(slot_ref.shape, F32)
    copies = []
    for i in range(CHUNKS):
        span = pl.ds(i * block * given, block * given)
        wide_ref[span, :] = back_ref[span, :].astype(F32)
        for p in range(i * block, (i + 1) * block):
            start = p * given
            out_ref[p] = wide_ref[start : start + out_depth, :].astype(BF16)
            start += out_depth
            val_ref[p] = wide_ref[start : start + val_depth, :].astype(BF16)
            start += val_depth
            spread = jnp.sum(wide_ref[start : start + 2, :], axis=1, keepdims=True)
            total = total + spread * choice_ref[p]
        for n, (ref, target) in enumerate(((out_ref, out_hbm), (val_ref, val_hbm))):
            copy = pltpu.make_async_copy(chunk_of(ref, i), chunk_of(target, i), sems.at[n, i])
            copy.start()
            copies.append(copy)
    slot_ref[...] = total
    for copy in copies:
        copy.wait()


def finish(back, choice, out_depth, val_depth, given):
    heads = choice.shape[0]
    shapes = [(heads, rows, LANES) for rows in (out_depth, val_depth)]
    return pl.pallas_call(
        functools.partial(finish_kernel, given),
        in_specs=[VMEM, VMEM],
        out_specs=[HBM, HBM, VMEM],
        out_shape=[jax.ShapeDtypeStruct(shape, BF16) for shape in shapes] + [jax.ShapeDtypeStruct((2, LANES), F32)],
        scratch_shapes=[pltpu.VMEM(back.shape, F32)]
        + [pltpu.VMEM(shape, BF16) for shape in shapes]
        + [pltpu.SemaphoreType.DMA((2, CHUNKS))],
        compiler_params=pltpu.CompilerParams(vmem_limit_bytes=24 * 1024 * 1024),
        name="finish",
    )(back, choice)


def slot_choice(table, owner):
    mine = (table == owner).astype(jnp.int32)
    heads = mine.shape[1]
    index = lax.iota(jnp.int32, heads)
    earlier = (index[None, :] < index[:, None]).astype(jnp.int32)
    rank = jnp.sum(earlier[None] * mine[:, None, :], axis=2)
    lane = lax.iota(jnp.int32, LANES)
    chosen = (mine[:, :, None] == 1) & (rank[:, :, None] == lane[None, None, :])
    return chosen.astype(F32).transpose(1, 0, 2)


def body(output_grad, output_momentum, values_grad, values_momentum, owner_table):
    owners, layers = lax.axis_size("dp"), lax.axis_size("layer")
    out_rows, out_columns = output_grad.shape[2:]
    val_rows, val_columns = values_grad.shape[2:]
    capacity = 3
    out_grad, out_momentum = flat(output_grad[0]), flat(output_momentum[0])
    val_grad, val_momentum = flat(values_grad[0]), flat(values_momentum[0])
    heads = out_grad.shape[0]

    everyone = owners * layers
    parts = lax.all_to_all(
        local_squares(out_grad, val_grad, owners).reshape(owners, 1, LANES),
        "dp",
        split_axis=0,
        concat_axis=0,
        tiled=True,
    ).reshape(owners, LANES)
    mine = row_sum(parts)
    mine, *momenta = lax.optimization_barrier((mine, out_momentum, val_momentum))
    decayed = prepare(*momenta)
    parts = [mine] + [
        lax.ppermute(mine, "layer", [(i, (i + shift) % layers) for i in range(layers)]) for shift in range(1, layers)
    ]
    count = (output_grad.size + values_grad.size) * everyone

    send, clip = rows_to_send(parts, count, out_grad, val_grad, decayed)
    out_next, val_next = next_momentum(clip, out_grad, out_momentum, val_grad, val_momentum)
    got = lax.all_to_all(send, "dp", split_axis=0, concat_axis=0, tiled=True)

    out_depth, val_depth = out_grad.shape[1], val_grad.shape[1]
    given = out_depth + val_depth + 2
    back = orthogonalize(got, ((out_rows, out_columns), (val_rows, val_columns)), given)
    back = lax.all_to_all(
        back.reshape(heads, given // 2, 2, LANES), "dp", split_axis=0, concat_axis=0, tiled=True
    )
    choice = slot_choice(owner_table[0, :, :, 0], lax.axis_index("dp"))
    out_update, val_update, slots = finish(
        back.reshape(heads * given, LANES), choice, out_depth, val_depth, given
    )

    return (
        unflat(out_update.reshape(out_grad.shape), out_rows)[None],
        unflat(out_next, out_rows)[None],
        unflat(val_update.reshape(val_grad.shape), val_rows)[None],
        unflat(val_next, val_rows)[None],
        slots[None, :, None, :capacity],
    )


def solution(mesh):
    rows = P("layer", None, "dp", None)
    return jax.shard_map(
        body,
        mesh=mesh,
        in_specs=(rows, rows, rows, rows, P("layer", None, None, None)),
        out_specs=(rows, rows, rows, rows, rows),
        check_vma=False,
    )
```

```python
import functools
import math

import jax
import jax.numpy as jnp
from jax import lax
from jax.experimental import pallas as pl
from jax.experimental.pallas import tpu as pltpu
from jax.sharding import PartitionSpec as P

MOMENT = 0.95
COEF_A = 3.4445
COEF_B = -4.775
COEF_C = 2.0315
CLIP_RMS = 0.5
LANES = 128
F32 = jnp.float32
BF16 = jnp.bfloat16


def flat(x):
    heads, rows, columns = x.shape
    x = x.reshape(heads, rows, columns // LANES, LANES).transpose(0, 2, 1, 3)
    return x.reshape(heads, rows * columns // LANES, LANES)


def unflat(x, rows):
    heads, depth, _ = x.shape
    x = x.reshape(heads, depth // rows, rows, LANES).transpose(0, 2, 1, 3)
    return x.reshape(heads, rows, depth // rows * LANES)


HBM = pl.BlockSpec(memory_space=pltpu.HBM)
VMEM = pl.BlockSpec(memory_space=pltpu.VMEM)
CHUNKS = 8
GRANT = 60 * 1024 * 1024
ORTHO = 40 * 1024 * 1024


def chunk_of(ref, i):
    block = ref.shape[0] // CHUNKS
    return ref.at[pl.ds(i * block, block)]


def loads(pairs, sems):
    copies = []
    for i in range(CHUNKS):
        row = []
        for n, (source, target) in enumerate(pairs):
            copy = pltpu.make_async_copy(chunk_of(source, i), chunk_of(target, i), sems.at[n, i])
            copy.start()
            row.append(copy)
        copies.append(row)
    return copies


def squares_kernel(out_hbm, val_hbm, sum_ref, out_ref, val_ref, sems):
    copies = loads([(out_hbm, out_ref), (val_hbm, val_ref)], sems)
    total = jnp.zeros((8, LANES), F32)
    for i, row in enumerate(copies):
        for copy, ref in zip(row, (out_ref, val_ref)):
            copy.wait()
            wide = chunk_of(ref, i)[...].astype(F32).reshape(-1, 8, LANES)
            total = total + jnp.sum(wide * wide, axis=0)
    sum_ref[...] = jnp.broadcast_to(jnp.sum(total, axis=0, keepdims=True), sum_ref.shape)


def local_squares(out_grad, val_grad, pieces):
    return pl.pallas_call(
        squares_kernel,
        in_specs=[HBM, HBM],
        out_specs=[VMEM] * 3,
        out_shape=[pltpu.VMEM((pieces, LANES), F32)] + [pltpu.VMEM(x.shape, BF16) for x in (out_grad, val_grad)],
        scratch_shapes=[pltpu.SemaphoreType.DMA((2, CHUNKS))],
        compiler_params=pltpu.CompilerParams(vmem_limit_bytes=16 * 1024 * 1024),
        name="squares",
    )(*(pltpu.with_memory_space_constraint(x, pltpu.HBM) for x in (out_grad, val_grad)))


def prepare_kernel(om_ref, vm_ref, decayed_ref):
    depth = om_ref.shape[1]
    decayed_ref[:, :depth, :] = (MOMENT * MOMENT) * om_ref[...]
    decayed_ref[:, depth:, :] = (MOMENT * MOMENT) * vm_ref[...]


def prepare(out_momentum, val_momentum):
    heads = out_momentum.shape[0]
    depth = out_momentum.shape[1] + val_momentum.shape[1]
    return pl.pallas_call(
        prepare_kernel,
        in_specs=[VMEM, VMEM],
        out_specs=VMEM,
        out_shape=jax.ShapeDtypeStruct((heads, depth, LANES), F32),
        compiler_params=pltpu.CompilerParams(vmem_limit_bytes=16 * 1024 * 1024),
        name="prepare",
    )(out_momentum, val_momentum)


def row_sum_kernel(parts_ref, sum_ref):
    sum_ref[...] = jnp.broadcast_to(jnp.sum(parts_ref[...], axis=0, keepdims=True), sum_ref.shape)


def row_sum(parts):
    return pl.pallas_call(
        row_sum_kernel,
        in_specs=[VMEM],
        out_specs=VMEM,
        out_shape=jax.ShapeDtypeStruct((8, LANES), F32),
        compiler_params=pltpu.CompilerParams(vmem_limit_bytes=4 * 1024 * 1024),
        name="row_sum",
    )(parts)


def clip_of(parts, count):
    total = jnp.sum(jnp.sum(parts, axis=0, keepdims=True), axis=1, keepdims=True)
    return jnp.minimum(1.0, CLIP_RMS * math.sqrt(count) / jnp.sqrt(total + 1e-06))


def send_kernel(count, layers, *refs):
    parts_refs, refs = refs[:layers], refs[layers:]
    og_ref, vg_ref, decayed_ref, send_ref, clip_hbm, clip_ref, clip_sem = refs
    parts = jnp.concatenate([ref[0:1, :] for ref in parts_refs], axis=0)
    clip = jnp.broadcast_to(clip_of(parts, count), clip_ref.shape)
    clip_ref[...] = clip
    copy = pltpu.make_async_copy(clip_ref, clip_hbm, clip_sem)
    copy.start()
    factor = ((1.0 + MOMENT) * clip[0:1]).reshape(1, 1, LANES)
    depth = og_ref.shape[1]
    send_ref[:, :depth, :] = (factor * og_ref[...].astype(F32) + decayed_ref[:, :depth, :]).astype(BF16)
    send_ref[:, depth:, :] = (factor * vg_ref[...].astype(F32) + decayed_ref[:, depth:, :]).astype(BF16)
    copy.wait()


def rows_to_send(parts, count, out_grad, val_grad, decayed):
    return pl.pallas_call(
        functools.partial(send_kernel, count, len(parts)),
        in_specs=[VMEM] * (len(parts) + 3),
        out_specs=[VMEM, HBM],
        out_shape=[jax.ShapeDtypeStruct(decayed.shape, BF16), pltpu.HBM((8, LANES), F32)],
        scratch_shapes=[pltpu.VMEM((8, LANES), F32), pltpu.SemaphoreType.DMA(())],
        compiler_params=pltpu.CompilerParams(vmem_limit_bytes=24 * 1024 * 1024),
        name="send",
    )(*parts, out_grad, val_grad, decayed)


def next_kernel(clip_ref, og_ref, om_ref, vg_ref, vm_ref, on_ref, vn_ref):
    clip = clip_ref[0:1, :].reshape(1, 1, LANES)
    on_ref[...] = MOMENT * om_ref[...] + clip * og_ref[...].astype(F32)
    vn_ref[...] = MOMENT * vm_ref[...] + clip * vg_ref[...].astype(F32)


def next_momentum(clip, out_grad, out_momentum, val_grad, val_momentum, steps=8):
    heads = out_grad.shape[0]
    block = heads // steps

    def spec(x):
        return pl.BlockSpec((block,) + x.shape[1:], lambda i: (i, 0, 0))

    return pl.pallas_call(
        next_kernel,
        grid=(steps,),
        in_specs=[pl.BlockSpec((8, LANES), lambda i: (0, 0))]
        + [spec(x) for x in (out_grad, out_momentum, val_grad, val_momentum)],
        out_specs=[spec(out_grad), spec(val_grad)],
        out_shape=[jax.ShapeDtypeStruct(x.shape, F32) for x in (out_grad, val_grad)],
        name="next",
    )(clip, out_grad, out_momentum, val_grad, val_momentum)


def dot(a, b):
    return lax.dot_general(a.astype(BF16), b.astype(BF16), (((1,), (0,)), ((), ())), preferred_element_type=F32)


def polynomials(grams):
    every, scales = [], []
    for gram in grams:
        rows = lax.broadcasted_iota(jnp.int32, gram.shape, 0)
        columns = lax.broadcasted_iota(jnp.int32, gram.shape, 1)
        diagonal = jnp.where(rows == columns, gram, 0.0)
        squares = jnp.sum(jnp.sum(diagonal, axis=0, keepdims=True), axis=1, keepdims=True)
        every.append(squares)
        scales.append(1.0 / (jnp.sqrt(squares) + 1e-07))
    grams = [(gram * scale) * scale for gram, scale in zip(grams, scales)]
    first = [COEF_B * gram + COEF_C * dot(gram, gram) for gram in grams]
    bent = [dot(f, gram) for f, gram in zip(first, grams)]
    grams = [
        COEF_A * COEF_A * gram + 2.0 * COEF_A * b + dot(f, b) for f, gram, b in zip(first, grams, bent)
    ]
    second = [COEF_B * gram + COEF_C * dot(gram, gram) for gram in grams]
    return every, scales, [COEF_A * (f + g) + dot(g, f) for f, g in zip(first, second)]


def thirds(value):
    high = value.astype(BF16).astype(F32)
    middle = (value - high).astype(BF16).astype(F32)
    low = value - high - middle
    lane = lax.broadcasted_iota(jnp.int32, (1, LANES), 1)
    return jnp.where(lane == 0, high, jnp.where(lane == 1, middle, jnp.where(lane == 2, low, 0.0)))


def orthogonal_kernel(sizes, got_ref, back_hbm, wide_ref, back_ref, out_ref, val_ref, sems):
    sources, depth, _ = got_ref.shape
    pitch, given = wide_ref.shape[0] // sources, back_ref.shape[0] // sources
    matrices = [(ref, rows, columns) for ref, (rows, columns) in zip((out_ref, val_ref), sizes)]
    for s in range(sources):
        wide_ref[s * pitch : s * pitch + depth, :] = got_ref[s].astype(F32)

    offset = 0
    grams = []
    for ref, rows, columns in matrices:
        for j in range(columns // LANES):
            parts = [
                wide_ref[pl.ds(offset + j * rows + r, sources, stride=pitch), :].astype(BF16) for r in range(rows)
            ]
            ref[:, j * LANES : (j + 1) * LANES] = jnp.concatenate(parts, axis=0)
        offset += columns // LANES * rows
        whole = ref[...]
        grams.append(lax.dot_general(whole, whole, (((1,), (1,)), ((), ())), preferred_element_type=F32))
    squares, scales, factors = polynomials(grams)

    offset = 0
    for (ref, rows, columns), scale, factor in zip(matrices, scales, factors):
        factor = factor.astype(BF16)
        final = scale * math.sqrt(max(rows * sources, columns))
        width = 512
        for at in range(0, columns, width):
            piece = ref[:, at : at + width]
            product = lax.dot_general(factor, piece, (((1,), (0,)), ((), ())), preferred_element_type=F32)
            product = final * (COEF_A * COEF_A * piece.astype(F32) + product)
            for k in range(width // LANES):
                j = at // LANES + k
                for r in range(rows):
                    wide_ref[pl.ds(offset + j * rows + r, sources, stride=given), :] = product[
                        r * sources : (r + 1) * sources, k * LANES : (k + 1) * LANES
                    ]
        offset += columns // LANES * rows

    for r, ((_, rows, columns), square) in enumerate(zip(matrices, squares)):
        spread = jnp.sqrt(square / (rows * sources * columns))
        wide_ref[pl.ds(offset + r, sources, stride=given), :] = jnp.broadcast_to(thirds(spread), (sources, LANES))

    copies = []
    for i in range(CHUNKS):
        block = back_ref.shape[0] // CHUNKS
        back_ref[i * block : (i + 1) * block, :] = wide_ref[i * block : (i + 1) * block, :].astype(BF16)
        copy = pltpu.make_async_copy(chunk_of(back_ref, i), chunk_of(back_hbm, i), sems.at[i])
        copy.start()
        copies.append(copy)
    for copy in copies:
        copy.wait()


def orthogonalize(got, sizes, given, pitch=136):
    sources = got.shape[0]
    return pl.pallas_call(
        functools.partial(orthogonal_kernel, sizes),
        in_specs=[VMEM],
        out_specs=HBM,
        out_shape=pltpu.HBM((sources * given, LANES), BF16),
        scratch_shapes=[pltpu.VMEM((sources * pitch, LANES), F32), pltpu.VMEM((sources * given, LANES), BF16)]
        + [pltpu.VMEM((rows * sources, columns), BF16) for rows, columns in sizes]
        + [pltpu.SemaphoreType.DMA((CHUNKS,))],
        compiler_params=pltpu.CompilerParams(vmem_limit_bytes=ORTHO),
        name="orthogonal",
    )(got)


def finish_kernel(given, back_ref, choice_ref, out_hbm, val_hbm, slot_ref, wide_ref, out_ref, val_ref, sems):
    heads, out_depth, _ = out_ref.shape
    val_depth = val_ref.shape[1]
    block = heads // CHUNKS
    total = jnp.zeros(slot_ref.shape, F32)
    copies = []
    for i in range(CHUNKS):
        span = pl.ds(i * block * given, block * given)
        wide_ref[span, :] = back_ref[span, :].astype(F32)
        for p in range(i * block, (i + 1) * block):
            start = p * given
            out_ref[p] = wide_ref[start : start + out_depth, :].astype(BF16)
            start += out_depth
            val_ref[p] = wide_ref[start : start + val_depth, :].astype(BF16)
            start += val_depth
            spread = jnp.sum(wide_ref[start : start + 2, :], axis=1, keepdims=True)
            total = total + spread * choice_ref[p]
        for n, (ref, target) in enumerate(((out_ref, out_hbm), (val_ref, val_hbm))):
            copy = pltpu.make_async_copy(chunk_of(ref, i), chunk_of(target, i), sems.at[n, i])
            copy.start()
            copies.append(copy)
    slot_ref[...] = total
    for copy in copies:
        copy.wait()


def finish(back, choice, out_depth, val_depth, given):
    heads = choice.shape[0]
    shapes = [(heads, rows, LANES) for rows in (out_depth, val_depth)]
    return pl.pallas_call(
        functools.partial(finish_kernel, given),
        in_specs=[VMEM, VMEM],
        out_specs=[HBM, HBM, VMEM],
        out_shape=[jax.ShapeDtypeStruct(shape, BF16) for shape in shapes] + [jax.ShapeDtypeStruct((2, LANES), F32)],
        scratch_shapes=[pltpu.VMEM(back.shape, F32)]
        + [pltpu.VMEM(shape, BF16) for shape in shapes]
        + [pltpu.SemaphoreType.DMA((2, CHUNKS))],
        compiler_params=pltpu.CompilerParams(vmem_limit_bytes=24 * 1024 * 1024),
        name="finish",
    )(back, choice)


def slot_choice(table, owner):
    mine = (table == owner).astype(jnp.int32)
    heads = mine.shape[1]
    index = lax.iota(jnp.int32, heads)
    earlier = (index[None, :] < index[:, None]).astype(jnp.int32)
    rank = jnp.sum(earlier[None] * mine[:, None, :], axis=2)
    lane = lax.iota(jnp.int32, LANES)
    chosen = (mine[:, :, None] == 1) & (rank[:, :, None] == lane[None, None, :])
    return chosen.astype(F32).transpose(1, 0, 2)


def body(output_grad, output_momentum, values_grad, values_momentum, owner_table):
    owners, layers = lax.axis_size("dp"), lax.axis_size("layer")
    out_rows, out_columns = output_grad.shape[2:]
    val_rows, val_columns = values_grad.shape[2:]
    capacity = 3
    out_grad, out_momentum = flat(output_grad[0]), flat(output_momentum[0])
    val_grad, val_momentum = flat(values_grad[0]), flat(values_momentum[0])
    heads = out_grad.shape[0]

    everyone = owners * layers
    squares, out_near, val_near = local_squares(out_grad, val_grad, owners)
    parts = lax.all_to_all(
        squares.reshape(owners, 1, LANES),
        "dp",
        split_axis=0,
        concat_axis=0,
        tiled=True,
    ).reshape(owners, LANES)
    mine = row_sum(parts)
    mine, *momenta = lax.optimization_barrier((mine, out_momentum, val_momentum))
    decayed = prepare(*momenta)
    parts = [mine] + [
        lax.ppermute(mine, "layer", [(i, (i + shift) % layers) for i in range(layers)]) for shift in range(1, layers)
    ]
    count = (output_grad.size + values_grad.size) * everyone

    send, clip = rows_to_send(parts, count, out_near, val_near, decayed)
    out_next, val_next = next_momentum(clip, out_grad, out_momentum, val_grad, val_momentum)
    got = lax.all_to_all(send, "dp", split_axis=0, concat_axis=0, tiled=True)

    out_depth, val_depth = out_grad.shape[1], val_grad.shape[1]
    given = out_depth + val_depth + 2
    back = orthogonalize(got, ((out_rows, out_columns), (val_rows, val_columns)), given)
    back = lax.all_to_all(
        back.reshape(heads, given // 2, 2, LANES), "dp", split_axis=0, concat_axis=0, tiled=True
    )
    choice = slot_choice(owner_table[0, :, :, 0], lax.axis_index("dp"))
    out_update, val_update, slots = finish(
        back.reshape(heads * given, LANES), choice, out_depth, val_depth, given
    )

    return (
        unflat(out_update.reshape(out_grad.shape), out_rows)[None],
        unflat(out_next, out_rows)[None],
        unflat(val_update.reshape(val_grad.shape), val_rows)[None],
        unflat(val_next, val_rows)[None],
        slots[None, :, None, :capacity],
    )


def solution(mesh):
    rows = P("layer", None, "dp", None)
    return jax.shard_map(
        body,
        mesh=mesh,
        in_specs=(rows, rows, rows, rows, P("layer", None, None, None)),
        out_specs=(rows, rows, rows, rows, rows),
        check_vma=False,
    )
```

```python
import functools
import math

import jax
import jax.numpy as jnp
from jax import lax
from jax.experimental import pallas as pl
from jax.experimental.pallas import tpu as pltpu
from jax.sharding import PartitionSpec as P

MOMENT = 0.95
COEF_A = 3.4445
COEF_B = -4.775
COEF_C = 2.0315
CLIP_RMS = 0.5
LANES = 128
F32 = jnp.float32
BF16 = jnp.bfloat16


def flat(x):
    heads, rows, columns = x.shape
    x = x.reshape(heads, rows, columns // LANES, LANES).transpose(0, 2, 1, 3)
    return x.reshape(heads, rows * columns // LANES, LANES)


def unflat(x, rows):
    heads, depth, _ = x.shape
    x = x.reshape(heads, depth // rows, rows, LANES).transpose(0, 2, 1, 3)
    return x.reshape(heads, rows, depth // rows * LANES)


HBM = pl.BlockSpec(memory_space=pltpu.HBM)
VMEM = pl.BlockSpec(memory_space=pltpu.VMEM)
CHUNKS = 8
PITCH = 136
GRANT = 60 * 1024 * 1024
ORTHO = 40 * 1024 * 1024


def chunk_of(ref, i):
    block = ref.shape[0] // CHUNKS
    return ref.at[pl.ds(i * block, block)]


def loads(pairs, sems):
    copies = []
    for i in range(CHUNKS):
        row = []
        for n, (source, target) in enumerate(pairs):
            copy = pltpu.make_async_copy(chunk_of(source, i), chunk_of(target, i), sems.at[n, i])
            copy.start()
            row.append(copy)
        copies.append(row)
    return copies


def squares_kernel(out_hbm, val_hbm, sum_ref, out_ref, val_ref, sems):
    copies = loads([(out_hbm, out_ref), (val_hbm, val_ref)], sems)
    total = jnp.zeros((8, LANES), F32)
    for i, row in enumerate(copies):
        for copy, ref in zip(row, (out_ref, val_ref)):
            copy.wait()
            wide = chunk_of(ref, i)[...].astype(F32).reshape(-1, 8, LANES)
            total = total + jnp.sum(wide * wide, axis=0)
    sum_ref[...] = jnp.broadcast_to(jnp.sum(total, axis=0, keepdims=True), sum_ref.shape)


def local_squares(out_grad, val_grad, pieces):
    return pl.pallas_call(
        squares_kernel,
        in_specs=[HBM, HBM],
        out_specs=[VMEM] * 3,
        out_shape=[pltpu.VMEM((pieces, LANES), F32)] + [pltpu.VMEM(x.shape, BF16) for x in (out_grad, val_grad)],
        scratch_shapes=[pltpu.SemaphoreType.DMA((2, CHUNKS))],
        compiler_params=pltpu.CompilerParams(vmem_limit_bytes=16 * 1024 * 1024),
        name="squares",
    )(*(pltpu.with_memory_space_constraint(x, pltpu.HBM) for x in (out_grad, val_grad)))


def prepare_kernel(om_ref, vm_ref, decayed_ref):
    depth = om_ref.shape[1]
    decayed_ref[:, :depth, :] = (MOMENT * MOMENT) * om_ref[...]
    decayed_ref[:, depth:, :] = (MOMENT * MOMENT) * vm_ref[...]


def prepare(out_momentum, val_momentum):
    heads = out_momentum.shape[0]
    depth = out_momentum.shape[1] + val_momentum.shape[1]
    return pl.pallas_call(
        prepare_kernel,
        in_specs=[VMEM, VMEM],
        out_specs=VMEM,
        out_shape=jax.ShapeDtypeStruct((heads, depth, LANES), F32),
        compiler_params=pltpu.CompilerParams(vmem_limit_bytes=16 * 1024 * 1024),
        name="prepare",
    )(out_momentum, val_momentum)


def row_sum_kernel(parts_ref, sum_ref):
    sum_ref[...] = jnp.broadcast_to(jnp.sum(parts_ref[...], axis=0, keepdims=True), sum_ref.shape)


def row_sum(parts):
    return pl.pallas_call(
        row_sum_kernel,
        in_specs=[VMEM],
        out_specs=VMEM,
        out_shape=jax.ShapeDtypeStruct((8, LANES), F32),
        compiler_params=pltpu.CompilerParams(vmem_limit_bytes=4 * 1024 * 1024),
        name="row_sum",
    )(parts)


def clip_of(parts, count):
    total = jnp.sum(jnp.sum(parts, axis=0, keepdims=True), axis=1, keepdims=True)
    return jnp.minimum(1.0, CLIP_RMS * math.sqrt(count) / jnp.sqrt(total + 1e-06))


def send_kernel(count, layers, *refs):
    parts_refs, refs = refs[:layers], refs[layers:]
    og_ref, vg_ref, decayed_ref, send_ref, clip_hbm, clip_ref, clip_sem = refs
    parts = jnp.concatenate([ref[0:1, :] for ref in parts_refs], axis=0)
    clip = jnp.broadcast_to(clip_of(parts, count), clip_ref.shape)
    clip_ref[...] = clip
    copy = pltpu.make_async_copy(clip_ref, clip_hbm, clip_sem)
    copy.start()
    factor = ((1.0 + MOMENT) * clip[0:1]).reshape(1, 1, LANES)
    depth = og_ref.shape[1]
    send_ref[:, :depth, :] = (factor * og_ref[...].astype(F32) + decayed_ref[:, :depth, :]).astype(BF16)
    send_ref[:, depth:, :] = (factor * vg_ref[...].astype(F32) + decayed_ref[:, depth:, :]).astype(BF16)
    copy.wait()


def rows_to_send(parts, count, out_grad, val_grad, decayed):
    return pl.pallas_call(
        functools.partial(send_kernel, count, len(parts)),
        in_specs=[VMEM] * (len(parts) + 3),
        out_specs=[VMEM, HBM],
        out_shape=[jax.ShapeDtypeStruct(decayed.shape, BF16), pltpu.HBM((8, LANES), F32)],
        scratch_shapes=[pltpu.VMEM((8, LANES), F32), pltpu.SemaphoreType.DMA(())],
        compiler_params=pltpu.CompilerParams(vmem_limit_bytes=24 * 1024 * 1024),
        name="send",
    )(*parts, out_grad, val_grad, decayed)


def next_kernel(clip_ref, og_ref, om_ref, vg_ref, vm_ref, on_ref, vn_ref):
    clip = clip_ref[0:1, :].reshape(1, 1, LANES)
    on_ref[...] = MOMENT * om_ref[...] + clip * og_ref[...].astype(F32)
    vn_ref[...] = MOMENT * vm_ref[...] + clip * vg_ref[...].astype(F32)


def next_momentum(clip, out_grad, out_momentum, val_grad, val_momentum, steps=8):
    heads = out_grad.shape[0]
    block = heads // steps

    def spec(x):
        return pl.BlockSpec((block,) + x.shape[1:], lambda i: (i, 0, 0))

    return pl.pallas_call(
        next_kernel,
        grid=(steps,),
        in_specs=[pl.BlockSpec((8, LANES), lambda i: (0, 0))]
        + [spec(x) for x in (out_grad, out_momentum, val_grad, val_momentum)],
        out_specs=[spec(out_grad), spec(val_grad)],
        out_shape=[jax.ShapeDtypeStruct(x.shape, F32) for x in (out_grad, val_grad)],
        name="next",
    )(clip, out_grad, out_momentum, val_grad, val_momentum)


def dot(a, b):
    return lax.dot_general(a.astype(BF16), b.astype(BF16), (((1,), (0,)), ((), ())), preferred_element_type=F32)


def polynomials(grams):
    every, scales = [], []
    for gram in grams:
        rows = lax.broadcasted_iota(jnp.int32, gram.shape, 0)
        columns = lax.broadcasted_iota(jnp.int32, gram.shape, 1)
        diagonal = jnp.where(rows == columns, gram, 0.0)
        squares = jnp.sum(jnp.sum(diagonal, axis=0, keepdims=True), axis=1, keepdims=True)
        every.append(squares)
        scales.append(1.0 / (jnp.sqrt(squares) + 1e-07))
    grams = [(gram * scale) * scale for gram, scale in zip(grams, scales)]
    first = [COEF_B * gram + COEF_C * dot(gram, gram) for gram in grams]
    bent = [dot(f, gram) for f, gram in zip(first, grams)]
    grams = [
        COEF_A * COEF_A * gram + 2.0 * COEF_A * b + dot(f, b) for f, gram, b in zip(first, grams, bent)
    ]
    second = [COEF_B * gram + COEF_C * dot(gram, gram) for gram in grams]
    return every, scales, [COEF_A * (f + g) + dot(g, f) for f, g in zip(first, second)]


def thirds(value):
    high = value.astype(BF16).astype(F32)
    middle = (value - high).astype(BF16).astype(F32)
    low = value - high - middle
    lane = lax.broadcasted_iota(jnp.int32, (1, LANES), 1)
    return jnp.where(lane == 0, high, jnp.where(lane == 1, middle, jnp.where(lane == 2, low, 0.0)))


def orthogonal_kernel(sizes, got_ref, back_hbm, wide_ref, back_ref, out_ref, val_ref, sems):
    sources, depth, _ = got_ref.shape
    pitch, given = PITCH, back_ref.shape[0] // sources
    matrices = [(ref, rows, columns) for ref, (rows, columns) in zip((out_ref, val_ref), sizes)]
    for s in range(sources):
        wide_ref[s * pitch : s * pitch + depth, :] = got_ref[s].astype(F32)

    offset = 0
    grams = []
    for ref, rows, columns in matrices:
        for j in range(columns // LANES):
            parts = [
                wide_ref[pl.ds(offset + j * rows + r, sources, stride=pitch), :].astype(BF16) for r in range(rows)
            ]
            ref[:, j * LANES : (j + 1) * LANES] = jnp.concatenate(parts, axis=0)
        offset += columns // LANES * rows
        whole = ref[...]
        grams.append(lax.dot_general(whole, whole, (((1,), (1,)), ((), ())), preferred_element_type=F32))
    squares, scales, factors = polynomials(grams)

    offset = 0
    for (ref, rows, columns), scale, factor in zip(matrices, scales, factors):
        factor = factor.astype(BF16)
        final = scale * math.sqrt(max(rows * sources, columns))
        width = 512
        for at in range(0, columns, width):
            piece = ref[:, at : at + width]
            product = lax.dot_general(factor, piece, (((1,), (0,)), ((), ())), preferred_element_type=F32)
            product = final * (COEF_A * COEF_A * piece.astype(F32) + product)
            for k in range(width // LANES):
                j = at // LANES + k
                for r in range(rows):
                    wide_ref[pl.ds(offset + j * rows + r, sources, stride=given), :] = product[
                        r * sources : (r + 1) * sources, k * LANES : (k + 1) * LANES
                    ]
        offset += columns // LANES * rows

    for r, ((_, rows, columns), square) in enumerate(zip(matrices, squares)):
        spread = jnp.sqrt(square / (rows * sources * columns))
        wide_ref[pl.ds(offset + r, sources, stride=given), :] = jnp.broadcast_to(thirds(spread), (sources, LANES))

    copies = []
    for i in range(CHUNKS):
        block = back_ref.shape[0] // CHUNKS
        back_ref[i * block : (i + 1) * block, :] = wide_ref[i * block : (i + 1) * block, :].astype(BF16)
        copy = pltpu.make_async_copy(chunk_of(back_ref, i), chunk_of(back_hbm, i), sems.at[i])
        copy.start()
        copies.append(copy)
    for copy in copies:
        copy.wait()


def orthogonalize(got, sizes, given):
    sources = got.shape[0]
    return pl.pallas_call(
        functools.partial(orthogonal_kernel, sizes),
        in_specs=[VMEM],
        out_specs=HBM,
        out_shape=pltpu.HBM((sources * given, LANES), BF16),
        scratch_shapes=[pltpu.VMEM(((sources + 1) * PITCH, LANES), F32), pltpu.VMEM((sources * given, LANES), BF16)]
        + [pltpu.VMEM((rows * sources, columns), BF16) for rows, columns in sizes]
        + [pltpu.SemaphoreType.DMA((CHUNKS,))],
        compiler_params=pltpu.CompilerParams(vmem_limit_bytes=ORTHO),
        name="orthogonal",
    )(got)


def finish_kernel(given, back_ref, choice_ref, out_hbm, val_hbm, slot_ref, wide_ref, out_ref, val_ref, sems):
    heads, out_depth, _ = out_ref.shape
    val_depth = val_ref.shape[1]
    block = heads // CHUNKS
    total = jnp.zeros(slot_ref.shape, F32)
    copies = []
    for i in range(CHUNKS):
        span = pl.ds(i * block * given, block * given)
        wide_ref[span, :] = back_ref[span, :].astype(F32)
        for p in range(i * block, (i + 1) * block):
            start = p * given
            out_ref[p] = wide_ref[start : start + out_depth, :].astype(BF16)
            start += out_depth
            val_ref[p] = wide_ref[start : start + val_depth, :].astype(BF16)
            start += val_depth
            spread = jnp.sum(wide_ref[start : start + 2, :], axis=1, keepdims=True)
            total = total + spread * choice_ref[p]
        for n, (ref, target) in enumerate(((out_ref, out_hbm), (val_ref, val_hbm))):
            copy = pltpu.make_async_copy(chunk_of(ref, i), chunk_of(target, i), sems.at[n, i])
            copy.start()
            copies.append(copy)
    slot_ref[...] = total
    for copy in copies:
        copy.wait()


def finish(back, choice, out_depth, val_depth, given):
    heads = choice.shape[0]
    shapes = [(heads, rows, LANES) for rows in (out_depth, val_depth)]
    return pl.pallas_call(
        functools.partial(finish_kernel, given),
        in_specs=[VMEM, VMEM],
        out_specs=[HBM, HBM, VMEM],
        out_shape=[jax.ShapeDtypeStruct(shape, BF16) for shape in shapes] + [jax.ShapeDtypeStruct((2, LANES), F32)],
        scratch_shapes=[pltpu.VMEM(back.shape, F32)]
        + [pltpu.VMEM(shape, BF16) for shape in shapes]
        + [pltpu.SemaphoreType.DMA((2, CHUNKS))],
        compiler_params=pltpu.CompilerParams(vmem_limit_bytes=24 * 1024 * 1024),
        name="finish",
    )(back, choice)


def slot_choice(table, owner):
    mine = (table == owner).astype(jnp.int32)
    heads = mine.shape[1]
    index = lax.iota(jnp.int32, heads)
    earlier = (index[None, :] < index[:, None]).astype(jnp.int32)
    rank = jnp.sum(earlier[None] * mine[:, None, :], axis=2)
    lane = lax.iota(jnp.int32, LANES)
    chosen = (mine[:, :, None] == 1) & (rank[:, :, None] == lane[None, None, :])
    return chosen.astype(F32).transpose(1, 0, 2)


def body(output_grad, output_momentum, values_grad, values_momentum, owner_table):
    owners, layers = lax.axis_size("dp"), lax.axis_size("layer")
    out_rows, out_columns = output_grad.shape[2:]
    val_rows, val_columns = values_grad.shape[2:]
    capacity = 3
    out_grad, out_momentum = flat(output_grad[0]), flat(output_momentum[0])
    val_grad, val_momentum = flat(values_grad[0]), flat(values_momentum[0])
    heads = out_grad.shape[0]

    everyone = owners * layers
    squares, out_near, val_near = local_squares(out_grad, val_grad, owners)
    parts = lax.all_to_all(
        squares.reshape(owners, 1, LANES),
        "dp",
        split_axis=0,
        concat_axis=0,
        tiled=True,
    ).reshape(owners, LANES)
    mine = row_sum(parts)
    mine, *momenta = lax.optimization_barrier((mine, out_momentum, val_momentum))
    decayed = prepare(*momenta)
    parts = [mine] + [
        lax.ppermute(mine, "layer", [(i, (i + shift) % layers) for i in range(layers)]) for shift in range(1, layers)
    ]
    count = (output_grad.size + values_grad.size) * everyone

    send, clip = rows_to_send(parts, count, out_near, val_near, decayed)
    out_next, val_next = next_momentum(clip, out_grad, out_momentum, val_grad, val_momentum)
    got = lax.all_to_all(send, "dp", split_axis=0, concat_axis=0, tiled=True)

    out_depth, val_depth = out_grad.shape[1], val_grad.shape[1]
    given = out_depth + val_depth + 2
    back = orthogonalize(got, ((out_rows, out_columns), (val_rows, val_columns)), given)
    back = lax.all_to_all(
        back.reshape(heads, given // 2, 2, LANES), "dp", split_axis=0, concat_axis=0, tiled=True
    )
    choice = slot_choice(owner_table[0, :, :, 0], lax.axis_index("dp"))
    out_update, val_update, slots = finish(
        back.reshape(heads * given, LANES), choice, out_depth, val_depth, given
    )

    return (
        unflat(out_update.reshape(out_grad.shape), out_rows)[None],
        unflat(out_next, out_rows)[None],
        unflat(val_update.reshape(val_grad.shape), val_rows)[None],
        unflat(val_next, val_rows)[None],
        slots[None, :, None, :capacity],
    )


def solution(mesh):
    rows = P("layer", None, "dp", None)
    return jax.shard_map(
        body,
        mesh=mesh,
        in_specs=(rows, rows, rows, rows, P("layer", None, None, None)),
        out_specs=(rows, rows, rows, rows, rows),
        check_vma=False,
    )
```

```python
import functools
import math

import jax
import jax.numpy as jnp
from jax import lax
from jax.experimental import pallas as pl
from jax.experimental.pallas import tpu as pltpu
from jax.sharding import PartitionSpec as P

MOMENT = 0.95
COEF_A = 3.4445
COEF_B = -4.775
COEF_C = 2.0315
CLIP_RMS = 0.5
LANES = 128
F32 = jnp.float32
BF16 = jnp.bfloat16


def flat(x):
    heads, rows, columns = x.shape
    x = x.reshape(heads, rows, columns // LANES, LANES).transpose(0, 2, 1, 3)
    return x.reshape(heads, rows * columns // LANES, LANES)


def unflat(x, rows):
    heads, depth, _ = x.shape
    x = x.reshape(heads, depth // rows, rows, LANES).transpose(0, 2, 1, 3)
    return x.reshape(heads, rows, depth // rows * LANES)


HBM = pl.BlockSpec(memory_space=pltpu.HBM)
VMEM = pl.BlockSpec(memory_space=pltpu.VMEM)
CHUNKS = 8
PITCH = 136
GRANT = 60 * 1024 * 1024
ORTHO = 40 * 1024 * 1024


def chunk_of(ref, i):
    block = ref.shape[0] // CHUNKS
    return ref.at[pl.ds(i * block, block)]


def loads(pairs, sems):
    copies = []
    for i in range(CHUNKS):
        row = []
        for n, (source, target) in enumerate(pairs):
            copy = pltpu.make_async_copy(chunk_of(source, i), chunk_of(target, i), sems.at[n, i])
            copy.start()
            row.append(copy)
        copies.append(row)
    return copies


def squares_kernel(out_hbm, val_hbm, sum_ref, out_ref, val_ref, sems):
    copies = loads([(out_hbm, out_ref), (val_hbm, val_ref)], sems)
    total = jnp.zeros((8, LANES), F32)
    for i, row in enumerate(copies):
        for copy, ref in zip(row, (out_ref, val_ref)):
            copy.wait()
            wide = chunk_of(ref, i)[...].astype(F32).reshape(-1, 8, LANES)
            total = total + jnp.sum(wide * wide, axis=0)
    sum_ref[...] = jnp.broadcast_to(jnp.sum(total, axis=0, keepdims=True), sum_ref.shape)


def local_squares(out_grad, val_grad, pieces):
    return pl.pallas_call(
        squares_kernel,
        in_specs=[HBM, HBM],
        out_specs=[VMEM] * 3,
        out_shape=[pltpu.VMEM((pieces, LANES), F32)] + [pltpu.VMEM(x.shape, BF16) for x in (out_grad, val_grad)],
        scratch_shapes=[pltpu.SemaphoreType.DMA((2, CHUNKS))],
        compiler_params=pltpu.CompilerParams(vmem_limit_bytes=16 * 1024 * 1024),
        name="squares",
    )(*(pltpu.with_memory_space_constraint(x, pltpu.HBM) for x in (out_grad, val_grad)))


def prepare_kernel(om_ref, vm_ref, decayed_ref):
    depth = om_ref.shape[1]
    decayed_ref[:, :depth, :] = (MOMENT * MOMENT) * om_ref[...]
    decayed_ref[:, depth:, :] = (MOMENT * MOMENT) * vm_ref[...]


def prepare(out_momentum, val_momentum):
    heads = out_momentum.shape[0]
    depth = out_momentum.shape[1] + val_momentum.shape[1]
    return pl.pallas_call(
        prepare_kernel,
        in_specs=[VMEM, VMEM],
        out_specs=VMEM,
        out_shape=jax.ShapeDtypeStruct((heads, depth, LANES), F32),
        compiler_params=pltpu.CompilerParams(vmem_limit_bytes=16 * 1024 * 1024),
        name="prepare",
    )(out_momentum, val_momentum)


def row_sum_kernel(parts_ref, sum_ref):
    sum_ref[...] = jnp.broadcast_to(jnp.sum(parts_ref[...], axis=0, keepdims=True), sum_ref.shape)


def row_sum(parts):
    return pl.pallas_call(
        row_sum_kernel,
        in_specs=[VMEM],
        out_specs=VMEM,
        out_shape=jax.ShapeDtypeStruct((8, LANES), F32),
        compiler_params=pltpu.CompilerParams(vmem_limit_bytes=4 * 1024 * 1024),
        name="row_sum",
    )(parts)


def clip_of(parts, count):
    total = jnp.sum(jnp.sum(parts, axis=0, keepdims=True), axis=1, keepdims=True)
    return jnp.minimum(1.0, CLIP_RMS * math.sqrt(count) / jnp.sqrt(total + 1e-06))


def send_kernel(count, layers, *refs):
    parts_refs, refs = refs[:layers], refs[layers:]
    og_ref, vg_ref, decayed_ref, send_ref, clip_hbm, clip_ref, clip_sem = refs
    parts = jnp.concatenate([ref[0:1, :] for ref in parts_refs], axis=0)
    clip = jnp.broadcast_to(clip_of(parts, count), clip_ref.shape)
    clip_ref[...] = clip
    copy = pltpu.make_async_copy(clip_ref, clip_hbm, clip_sem)
    copy.start()
    factor = ((1.0 + MOMENT) * clip[0:1]).reshape(1, 1, LANES)
    depth = og_ref.shape[1]
    send_ref[:, :depth, :] = (factor * og_ref[...].astype(F32) + decayed_ref[:, :depth, :]).astype(BF16)
    send_ref[:, depth:, :] = (factor * vg_ref[...].astype(F32) + decayed_ref[:, depth:, :]).astype(BF16)
    copy.wait()


def rows_to_send(parts, count, out_grad, val_grad, decayed):
    return pl.pallas_call(
        functools.partial(send_kernel, count, len(parts)),
        in_specs=[VMEM] * (len(parts) + 3),
        out_specs=[VMEM, HBM],
        out_shape=[jax.ShapeDtypeStruct(decayed.shape, BF16), pltpu.HBM((8, LANES), F32)],
        scratch_shapes=[pltpu.VMEM((8, LANES), F32), pltpu.SemaphoreType.DMA(())],
        compiler_params=pltpu.CompilerParams(vmem_limit_bytes=24 * 1024 * 1024),
        name="send",
    )(*parts, out_grad, val_grad, decayed)


def next_kernel(clip_ref, og_ref, om_ref, vg_ref, vm_ref, on_ref, vn_ref):
    clip = clip_ref[0:1, :].reshape(1, 1, LANES)
    on_ref[...] = MOMENT * om_ref[...] + clip * og_ref[...].astype(F32)
    vn_ref[...] = MOMENT * vm_ref[...] + clip * vg_ref[...].astype(F32)


def next_momentum(clip, out_grad, out_momentum, val_grad, val_momentum, steps=8):
    heads = out_grad.shape[0]
    block = heads // steps

    def spec(x):
        return pl.BlockSpec((block,) + x.shape[1:], lambda i: (i, 0, 0))

    return pl.pallas_call(
        next_kernel,
        grid=(steps,),
        in_specs=[pl.BlockSpec((8, LANES), lambda i: (0, 0))]
        + [spec(x) for x in (out_grad, out_momentum, val_grad, val_momentum)],
        out_specs=[spec(out_grad), spec(val_grad)],
        out_shape=[jax.ShapeDtypeStruct(x.shape, F32) for x in (out_grad, val_grad)],
        name="next",
    )(clip, out_grad, out_momentum, val_grad, val_momentum)


def dot(a, b):
    return lax.dot_general(a.astype(BF16), b.astype(BF16), (((1,), (0,)), ((), ())), preferred_element_type=F32)


def polynomials(grams):
    every, scales = [], []
    for gram in grams:
        rows = lax.broadcasted_iota(jnp.int32, gram.shape, 0)
        columns = lax.broadcasted_iota(jnp.int32, gram.shape, 1)
        diagonal = jnp.where(rows == columns, gram, 0.0)
        squares = jnp.sum(jnp.sum(diagonal, axis=0, keepdims=True), axis=1, keepdims=True)
        every.append(squares)
        scales.append(1.0 / (jnp.sqrt(squares) + 1e-07))
    grams = [(gram * scale) * scale for gram, scale in zip(grams, scales)]
    first = [COEF_B * gram + COEF_C * dot(gram, gram) for gram in grams]
    bent = [dot(f, gram) for f, gram in zip(first, grams)]
    grams = [
        COEF_A * COEF_A * gram + 2.0 * COEF_A * b + dot(f, b) for f, gram, b in zip(first, grams, bent)
    ]
    second = [COEF_B * gram + COEF_C * dot(gram, gram) for gram in grams]
    return every, scales, [COEF_A * (f + g) + dot(g, f) for f, g in zip(first, second)]


def thirds(value):
    high = value.astype(BF16).astype(F32)
    middle = (value - high).astype(BF16).astype(F32)
    low = value - high - middle
    lane = lax.broadcasted_iota(jnp.int32, (1, LANES), 1)
    return jnp.where(lane == 0, high, jnp.where(lane == 1, middle, jnp.where(lane == 2, low, 0.0)))


def orthogonal_kernel(sizes, got_ref, back_hbm, wide_ref, back_ref, out_ref, val_ref, sems):
    sources, depth, _ = got_ref.shape
    pitch, given = PITCH, back_ref.shape[0] // sources
    matrices = [(ref, rows, columns) for ref, (rows, columns) in zip((out_ref, val_ref), sizes)]
    for s in range(sources):
        wide_ref[s * pitch : s * pitch + depth, :] = got_ref[s].astype(F32)

    offset = 0
    grams = []
    for ref, rows, columns in matrices:
        for j in range(columns // LANES):
            parts = [
                wide_ref[pl.ds(offset + j * rows + r, sources, stride=pitch), :].astype(BF16) for r in range(rows)
            ]
            ref[:, j * LANES : (j + 1) * LANES] = jnp.concatenate(parts, axis=0)
        offset += columns // LANES * rows
        whole = ref[...]
        grams.append(lax.dot_general(whole, whole, (((1,), (1,)), ((), ())), preferred_element_type=F32))
    squares, scales, factors = polynomials(grams)

    offset = 0
    for (ref, rows, columns), scale, factor in zip(matrices, scales, factors):
        factor = factor.astype(BF16)
        final = scale * math.sqrt(max(rows * sources, columns))
        width = 512
        for at in range(0, columns, width):
            piece = ref[:, at : at + width]
            product = lax.dot_general(factor, piece, (((1,), (0,)), ((), ())), preferred_element_type=F32)
            product = final * (COEF_A * COEF_A * piece.astype(F32) + product)
            for k in range(width // LANES):
                j = at // LANES + k
                for r in range(rows):
                    wide_ref[pl.ds(offset + j * rows + r, sources, stride=given), :] = product[
                        r * sources : (r + 1) * sources, k * LANES : (k + 1) * LANES
                    ]
        offset += columns // LANES * rows

    for r, ((_, rows, columns), square) in enumerate(zip(matrices, squares)):
        spread = jnp.sqrt(square / (rows * sources * columns))
        wide_ref[pl.ds(offset + r, sources, stride=given), :] = jnp.broadcast_to(thirds(spread), (sources, LANES))

    copies = []
    for i in range(CHUNKS):
        block = back_ref.shape[0] // CHUNKS
        back_ref[i * block : (i + 1) * block, :] = wide_ref[i * block : (i + 1) * block, :].astype(BF16)
        copy = pltpu.make_async_copy(chunk_of(back_ref, i), chunk_of(back_hbm, i), sems.at[i])
        copy.start()
        copies.append(copy)
    for copy in copies:
        copy.wait()


def orthogonalize(got, sizes, given):
    sources = got.shape[0]
    return pl.pallas_call(
        functools.partial(orthogonal_kernel, sizes),
        in_specs=[VMEM],
        out_specs=HBM,
        out_shape=pltpu.HBM((sources * given, LANES), BF16),
        scratch_shapes=[pltpu.VMEM(((sources + 1) * PITCH, LANES), F32), pltpu.VMEM((sources * given, LANES), BF16)]
        + [pltpu.VMEM((rows * sources, columns), BF16) for rows, columns in sizes]
        + [pltpu.SemaphoreType.DMA((CHUNKS,))],
        compiler_params=pltpu.CompilerParams(vmem_limit_bytes=ORTHO),
        name="orthogonal",
    )(got)


def finish_kernel(given, back_ref, choice_ref, out_hbm, val_hbm, slot_ref, wide_ref, out_ref, val_ref, sems):
    heads, out_depth, _ = out_ref.shape
    val_depth = val_ref.shape[1]
    block = heads // CHUNKS
    total = jnp.zeros(slot_ref.shape, F32)
    copies = []
    for i in range(CHUNKS):
        span = pl.ds(i * block * given, block * given)
        wide_ref[span, :] = back_ref[span, :].astype(F32)
        for p in range(i * block, (i + 1) * block):
            start = p * given
            out_ref[p] = wide_ref[start : start + out_depth, :].astype(BF16)
            start += out_depth
            val_ref[p] = wide_ref[start : start + val_depth, :].astype(BF16)
            start += val_depth
            spread = jnp.sum(wide_ref[start : start + 2, :], axis=1, keepdims=True)
            total = total + spread * choice_ref[p]
        for n, (ref, target) in enumerate(((out_ref, out_hbm), (val_ref, val_hbm))):
            copy = pltpu.make_async_copy(chunk_of(ref, i), chunk_of(target, i), sems.at[n, i])
            copy.start()
            copies.append(copy)
    slot_ref[...] = total
    for copy in copies:
        copy.wait()


def finish(back, choice, out_depth, val_depth, given):
    heads = choice.shape[0]
    shapes = [(heads, rows, LANES) for rows in (out_depth, val_depth)]
    return pl.pallas_call(
        functools.partial(finish_kernel, given),
        in_specs=[VMEM, VMEM],
        out_specs=[HBM, HBM, VMEM],
        out_shape=[jax.ShapeDtypeStruct(shape, BF16) for shape in shapes] + [jax.ShapeDtypeStruct((2, LANES), F32)],
        scratch_shapes=[pltpu.VMEM(back.shape, F32)]
        + [pltpu.VMEM(shape, BF16) for shape in shapes]
        + [pltpu.SemaphoreType.DMA((2, CHUNKS))],
        compiler_params=pltpu.CompilerParams(vmem_limit_bytes=24 * 1024 * 1024),
        name="finish",
    )(back, choice)


def slot_choice(table, owner):
    mine = (table == owner).astype(jnp.int32)
    heads = mine.shape[1]
    index = lax.iota(jnp.int32, heads)
    earlier = (index[None, :] < index[:, None]).astype(jnp.int32)
    rank = jnp.sum(earlier[None] * mine[:, None, :], axis=2)
    lane = lax.iota(jnp.int32, LANES)
    chosen = (mine[:, :, None] == 1) & (rank[:, :, None] == lane[None, None, :])
    return chosen.astype(F32).transpose(1, 0, 2)


def body(output_grad, output_momentum, values_grad, values_momentum, owner_table):
    owners, layers = lax.axis_size("dp"), lax.axis_size("layer")
    out_rows, out_columns = output_grad.shape[2:]
    val_rows, val_columns = values_grad.shape[2:]
    capacity = 3
    out_grad, out_momentum = flat(output_grad[0]), flat(output_momentum[0])
    val_grad, val_momentum = flat(values_grad[0]), flat(values_momentum[0])
    heads = out_grad.shape[0]

    everyone = owners * layers
    squares, out_near, val_near = local_squares(out_grad, val_grad, owners)
    parts = lax.all_to_all(
        squares.reshape(owners, 1, LANES),
        "dp",
        split_axis=0,
        concat_axis=0,
        tiled=True,
    ).reshape(owners, LANES)
    mine = row_sum(parts)
    mine, *momenta = lax.optimization_barrier((mine, out_momentum, val_momentum))
    decayed = prepare(*momenta)
    parts = [mine] + [
        lax.ppermute(mine, "layer", [(i, (i + shift) % layers) for i in range(layers)]) for shift in sorted(range(1, layers), key=lambda d: -min(d, layers - d))
    ]
    count = (output_grad.size + values_grad.size) * everyone

    send, clip = rows_to_send(parts, count, out_near, val_near, decayed)
    out_next, val_next = next_momentum(clip, out_grad, out_momentum, val_grad, val_momentum)
    got = lax.all_to_all(send, "dp", split_axis=0, concat_axis=0, tiled=True)

    out_depth, val_depth = out_grad.shape[1], val_grad.shape[1]
    given = out_depth + val_depth + 2
    back = orthogonalize(got, ((out_rows, out_columns), (val_rows, val_columns)), given)
    back = lax.all_to_all(
        back.reshape(heads, given // 2, 2, LANES), "dp", split_axis=0, concat_axis=0, tiled=True
    )
    choice = slot_choice(owner_table[0, :, :, 0], lax.axis_index("dp"))
    out_update, val_update, slots = finish(
        back.reshape(heads * given, LANES), choice, out_depth, val_depth, given
    )

    return (
        unflat(out_update.reshape(out_grad.shape), out_rows)[None],
        unflat(out_next, out_rows)[None],
        unflat(val_update.reshape(val_grad.shape), val_rows)[None],
        unflat(val_next, val_rows)[None],
        slots[None, :, None, :capacity],
    )


def solution(mesh):
    rows = P("layer", None, "dp", None)
    return jax.shard_map(
        body,
        mesh=mesh,
        in_specs=(rows, rows, rows, rows, P("layer", None, None, None)),
        out_specs=(rows, rows, rows, rows, rows),
        check_vma=False,
    )
```
